512 devices in a mesh: ha: 4 (over x), wa: 16 (over y, z_hi, core), ta: 8 (over z_lo).
Axes of the slice: x: 4, y: 4, z: 16 (z_hi: 2, z_lo: 8; z = z_hi * 8 + z_lo), core: 2. Of those that a mesh axis runs over, the one named last changes fastest.
Arguments:
- hidden_states: bfloat16 [2, 96, 128, 5120], P(None, 'ha', 'wa', 'ta'), may hold values from -60 to 60
- queries: bfloat16 [2, 96, 128, 5120], P(None, 'ha', 'wa', 'ta'), may hold values from -120 to 120
- keys_values: bfloat16 [2, 2, 96, 128, 5120], P(None, None, 'ha', 'wa', 'ta'), may hold values from -16 to 16
- out_weight: bfloat16 [5120, 5120], P('ta', 'wa'), may hold values from -0.078125 to 0.078125
- mod_table: float32 [50, 3, 5120], P(None, None, 'ta'), may hold values from -4 to 4
- windows: int32 [40, 2], P('ta'), may hold values from 0 to 1, as said below
- step_index: int32 [1], replicated, may hold values from 0 to 49
Outputs:
- residual_out: bfloat16 [2, 96, 128, 5120], P(None, 'ha', 'wa', 'ta')
- ffn_input: bfloat16 [2, 96, 128, 5120], P(None, 'ha', 'wa', 'ta')
The draws below stay inside these ranges and needn't reach their ends.
Inputs may be any that keep to these rules, and one draw needn't show every extreme that they name: `windows`: some head has both radii equal to 1.
All inputs are finite; a program needn't handle non-finite values.
Results may differ from the reference program's by a relative error of at most 0.0085.
Values may be sent and summed in bfloat16 or wider, within the bound.
A program may use at most 64 MiB of HBM per device.

```python
import math
import jax
import jax.numpy as jnp
from jax import lax

D = 5120
HEADS = 40
HD = 128
TILE = 8
FRAMES = 2
STEPS = 50
H = 96
W = 128
N_TA = 8


def base_keys(key):
    return jnp.clip(jax.random.normal(key, (FRAMES, H, W, HEADS * HD), jnp.float32), -4.0, 4.0)


def draw_queries(key, part):
    shared = base_keys(key)
    key = jax.random.fold_in(key, 5)
    result = jnp.clip(jax.random.normal(key, shared.shape, jnp.float32), -4.0, 4.0)
    return result.astype(jnp.bfloat16)


def draw_keys_values(key, part):
    shared = base_keys(key)
    key = jax.random.fold_in(key, 9)
    keys_part = shared
    values_part = 4.0 * jnp.clip(jax.random.normal(key, shared.shape, jnp.float32), -4.0, 4.0)
    return jnp.stack([keys_part, values_part], 0).astype(jnp.bfloat16)


def draw_hidden_states(key, part):
    key = jax.random.fold_in(key, 21)
    row_key = jax.random.fold_in(key, 1)
    col_key = jax.random.fold_in(key, 2)
    main_key = jax.random.fold_in(key, 4)
    shape = (FRAMES, H, W, D)
    row_scale = 10.0 ** jax.random.uniform(row_key, (FRAMES, H, W, 1), jnp.float32)
    position = lax.broadcasted_iota(jnp.float32, (D,), 0) / D
    col_scale = 0.05 * 3.0 ** position * 10.0 ** jax.random.uniform(col_key, (D,), jnp.float32)
    base = jnp.clip(jax.random.normal(main_key, shape, jnp.float32), -4.0, 4.0)
    return (base * row_scale * col_scale).astype(jnp.bfloat16)


def draw_windows(key, part):
    key = jax.random.fold_in(key, 13)
    radii = jax.random.randint(key, (HEADS, 2), 0, 2)
    picked = jax.random.randint(jax.random.fold_in(key, 1), (), 0, HEADS)
    head_ids = lax.broadcasted_iota(jnp.int32, (HEADS, 2), 0)
    return jnp.where(head_ids == picked, 1, radii).astype(jnp.int32)


def shard_levels(own_key, extent, cuts, smallest, high):
    def one(dim, parts):
        draws = jax.random.uniform(jax.random.fold_in(jax.random.fold_in(own_key, 6), dim), (parts,), jnp.float32, smallest / len(cuts), high / len(cuts))
        return jnp.repeat(jnp.exp(draws), extent[dim] // parts).reshape((-1,) + (1,) * (len(extent) - dim - 1))

    loudness = one(*cuts[0])
    for cut in cuts[1:]:
        loudness = loudness * one(*cut)
    return loudness


def normal_values(key, extent, width, most, cuts=(), held_as=jnp.bfloat16):
    gain = shard_levels(key, extent, cuts, -0.22, 0.18) if cuts else 1.0
    values = jax.random.normal(key, extent, jnp.float32) * width * gain
    return jnp.minimum(jnp.maximum(values, -most), most).astype(held_as)


def setup_inputs(seed: int = 0) -> dict:
    streams_of = jax.random.split(jax.random.key(seed), 8)
    hidden_states = draw_hidden_states(jax.random.fold_in(streams_of[7], 71), 0)
    queries = draw_queries(jax.random.fold_in(streams_of[7], 71), 0)
    keys_values = draw_keys_values(jax.random.fold_in(streams_of[7], 71), 0)
    out_weight = normal_values(streams_of[3], (HEADS * HD, D), (HEADS * HD) ** -0.5, 0.078125, ((0, 8), (1, 16)))
    mod_table = normal_values(streams_of[4], (STEPS, 3, D), 0.7, 4.0, ((2, 8),), jnp.float32)
    windows = draw_windows(jax.random.fold_in(streams_of[7], 71), 0)
    step_index = jax.random.randint(streams_of[6], (1,), 0, STEPS).astype(jnp.int32)
    return dict(hidden_states=hidden_states, queries=queries, keys_values=keys_values, out_weight=out_weight, mod_table=mod_table, windows=windows, step_index=step_index)


EPSILON = 1e-06

def tile_attention(queries, padded, windows, tile_index):
    tile_cols = W // TILE
    tile_rows = H // TILE
    tile_row = (tile_index // tile_cols).astype(jnp.int32)
    tile_col = (tile_index % tile_cols).astype(jnp.int32)
    zero = jnp.int32(0)
    span = 3 * TILE
    block = lax.dynamic_slice(queries, (zero, tile_row * TILE, tile_col * TILE, zero), (FRAMES, TILE, TILE, HEADS * HD))
    query_f = block.reshape(-1, HEADS, HD).astype(jnp.float32)
    near = lax.dynamic_slice(padded, (zero, zero, tile_row * TILE, tile_col * TILE, zero), (2, FRAMES, span, span, HEADS * HD))
    key_f = near[0].reshape(-1, HEADS, HD).astype(jnp.float32)
    value_f = near[1].reshape(-1, HEADS, HD).astype(jnp.float32)
    row_gap = (lax.broadcasted_iota(jnp.int32, (FRAMES, span, span), 1) // TILE - 1).reshape(-1)
    col_gap = (lax.broadcasted_iota(jnp.int32, (FRAMES, span, span), 2) // TILE - 1).reshape(-1)
    inside = (tile_row + row_gap >= 0) & (tile_row + row_gap < tile_rows) & (tile_col + col_gap >= 0) & (tile_col + col_gap < tile_cols)
    allowed = inside[None, :] & (jnp.abs(row_gap)[None, :] <= windows[:, 0:1]) & (jnp.abs(col_gap)[None, :] <= windows[:, 1:2])
    scale = 1.0 / math.sqrt(HD)
    scores = jnp.einsum('qhd,khd->hqk', query_f, key_f) * scale
    scores = jnp.where(allowed[:, None, :], scores, -jnp.inf)
    highest = lax.optimization_barrier(jnp.max(scores, axis=2, keepdims=True))
    expo = jnp.exp(scores - highest)
    total = lax.optimization_barrier(jnp.sum(expo, axis=2, keepdims=True))
    weights = (expo / total).astype(jnp.bfloat16)
    output = jnp.einsum('hqk,khd->qhd', weights.astype(jnp.float32), value_f)
    return output.astype(jnp.bfloat16).reshape(FRAMES * TILE * TILE, HEADS * HD)

def reference(hidden_states, queries, keys_values, out_weight, mod_table, windows, step_index):
    padded = jnp.pad(keys_values, ((0, 0), (0, 0), (TILE, TILE), (TILE, TILE), (0, 0)))
    tile_rows = H // TILE
    tile_cols = W // TILE
    tiles = lax.map(lambda index: tile_attention(queries, padded, windows, index), jnp.arange(tile_rows * tile_cols, dtype=jnp.int32))
    tiles = tiles.reshape(tile_rows, tile_cols, FRAMES, TILE, TILE, HEADS * HD)
    attention = jnp.transpose(tiles, (2, 0, 3, 1, 4, 5)).reshape(FRAMES * H * W, HEADS * HD)
    group_width = HEADS * HD // N_TA
    projected = jnp.zeros((FRAMES * H * W, D), jnp.float32)
    for group in range(N_TA):
        partial_sum = jnp.dot(attention[:, group * group_width:(group + 1) * group_width], out_weight[group * group_width:(group + 1) * group_width], preferred_element_type=jnp.float32).astype(jnp.bfloat16)
        partial_sum = lax.optimization_barrier(partial_sum)
        projected = projected + partial_sum.astype(jnp.float32)
    picked = lax.dynamic_index_in_dim(mod_table, step_index[0].astype(jnp.int32), 0, keepdims=False)
    mixed = hidden_states.reshape(-1, D).astype(jnp.float32) + picked[0] * projected
    average = lax.optimization_barrier(jnp.sum(mixed, axis=1, keepdims=True)) / D
    variance = lax.optimization_barrier(jnp.sum(mixed * mixed, axis=1, keepdims=True)) / D - average * average
    normed = (mixed - average) * lax.rsqrt(variance + EPSILON)
    ffn_input = (normed * (1.0 + picked[2]) + picked[1]).astype(jnp.bfloat16)
    residual_out = mixed.astype(jnp.bfloat16)
    return (residual_out.reshape(FRAMES, H, W, D), ffn_input.reshape(FRAMES, H, W, D))
```

```python
import math

import jax
import jax.numpy as jnp
from jax import lax
from jax.experimental import pallas as pl
from jax.experimental.pallas import tpu as pltpu
from jax.sharding import PartitionSpec as P

D = 5120
HD = 128
TILE = 8
EPSILON = 1e-06

N_HA, N_WA, N_TA = 4, 16, 8
N_Y = 4
FRAMES, ROWS, COLS = 2, 24, 8
FEAT = 640
HEADS_HERE = 5
T_ROWS = ROWS // TILE
TOK = FRAMES * TILE * TILE
HALF = TILE * TILE
TOKENS = T_ROWS * TOK
SHARD = D // N_WA
QUARTER = SHARD // N_HA
N_PIECE = N_TA * T_ROWS
MASKED = -1e30
MESH = pl.DeviceIdType.MESH
NT = (((1,), (1,)), ((), ()))


def kernel(
    win_ref,
    step_ref,
    hid_ref,
    q_ref,
    kv_ref,
    wt_ref,
    mod_ref,
    res_ref,
    ffn_ref,
    own,
    par,
    far,
    wall,
    hid,
    qry,
    mod,
    att,
    o_part,
    m_part,
    l_part,
    slot_r,
    slot_l,
    mixed,
    stat,
    lsem,
    ssem,
    rsem,
    ssem_r,
    rsem_r,
    ssem_l,
    rsem_l,
    ssem_s,
    rsem_s,
):
    x = lax.axis_index("ha")
    wa = lax.axis_index("wa")
    g = lax.axis_index("ta")
    y = wa // 4
    zh = lax.rem(wa // 2, 2)
    c = lax.rem(wa, 2)
    nw = 4 * y + 2 * (1 - zh) + c

    dev_par = (x, 4 * y + 2 * zh + 1 - c, g)
    dev_far = (x, lax.rem(wa + 15 + 2 * c, 16), g)
    dev_z = (x, nw, g)
    dev_x = [(lax.rem(x + j + 1, N_HA), wa, g) for j in range(3)]
    dev_y = [(x, lax.rem(wa + 4 * (j + 1), 16), g) for j in range(3)]
    dev_t = [(x, wa, lax.rem(g + j + 1, N_TA)) for j in range(7)]

    def shard_rows(index):
        return pl.ds(pl.multiple_of(index * SHARD, SHARD), SHARD)

    def quarter_rows(index, part):
        return pl.ds(pl.multiple_of(index * SHARD + part * QUARTER, QUARTER), QUARTER)

    loads = []
    for f in range(FRAMES):
        for r in range(T_ROWS):
            loads.append(
                pltpu.make_async_copy(
                    kv_ref.at[:, f, pl.ds(r * HALF, HALF), :],
                    own.at[:, pl.ds((r + 1) * TOK + f * HALF, HALF), :],
                    lsem.at[f * T_ROWS + r],
                )
            )
    load_w = pltpu.make_async_copy(wt_ref, wall.at[shard_rows(wa)], lsem.at[6])
    load_q = pltpu.make_async_copy(q_ref, qry, lsem.at[7])
    load_h = pltpu.make_async_copy(hid_ref, hid, lsem.at[8])
    load_m = pltpu.make_async_copy(mod_ref, mod, lsem.at[9])
    for load in loads:
        load.start()
    load_w.start()
    load_q.start()
    load_h.start()
    load_m.start()

    @pl.when(g == 0)
    def _():
        slot_r[...] = jnp.zeros_like(slot_r)

    @pl.when(g == N_TA - 1)
    def _():
        slot_l[...] = jnp.zeros_like(slot_l)

    barrier = pltpu.get_barrier_semaphore()
    peers = [dev_par, dev_far, dev_z] + dev_x + dev_y + dev_t
    for peer in peers:
        pl.semaphore_signal(barrier, inc=1, device_id=peer, device_id_type=MESH)
    for load in loads:
        load.wait()
    load_w.wait()
    pl.semaphore_wait(barrier, len(peers))

    def remote(index, src, dst, device):
        return pltpu.make_async_remote_copy(
            src_ref=src,
            dst_ref=dst,
            send_sem=ssem.at[index],
            recv_sem=rsem.at[index],
            device_id=device,
            device_id_type=MESH,
        )

    def rows(buf, first, count):
        return buf.at[:, pl.ds(first * TOK, count * TOK), :]

    w_z = remote(0, wall.at[quarter_rows(wa, x)], wall.at[quarter_rows(wa, x)], dev_z)
    far_a = remote(1, rows(own, 1, 1), rows(far, 1, 1), dev_far)
    far_b = remote(2, rows(own, 3, 1), rows(far, 3, 1), dev_far)
    far_c = remote(3, rows(own, 2, 1), rows(far, 2, 1), dev_far)
    up = remote(4, rows(own, 1, 1), rows(own, 4, 1), dev_x[2])
    down = remote(5, rows(own, 3, 1), rows(own, 0, 1), dev_x[0])
    par_mid = remote(6, rows(own, 1, 3), rows(par, 1, 3), dev_par)
    par_top = remote(7, rows(own, 0, 1), rows(par, 0, 1), dev_par)
    par_bot = remote(8, rows(own, 4, 1), rows(par, 4, 1), dev_par)
    far_up = remote(9, rows(far, 1, 1), rows(far, 4, 1), dev_x[2])
    far_down = remote(10, rows(far, 3, 1), rows(far, 0, 1), dev_x[0])
    w_x = [
        remote(11 + j, wall.at[quarter_rows(nw, x)], wall.at[quarter_rows(nw, x)], dev_x[j])
        for j in range(3)
    ]
    w_yn = [
        remote(14 + j, wall.at[shard_rows(wa)], wall.at[shard_rows(wa)], dev_y[j]) for j in range(3)
    ]
    w_yf = [
        remote(17 + j, wall.at[shard_rows(nw)], wall.at[shard_rows(nw)], dev_y[j]) for j in range(3)
    ]
    w_c = [
        remote(20, wall.at[shard_rows(wa)], wall.at[shard_rows(wa)], dev_par),
        remote(21, wall.at[shard_rows(nw)], wall.at[shard_rows(nw)], dev_par),
    ]
    for j in range(3):
        near = lax.rem(wa + 4 * (3 - j), 16)
        w_c.append(remote(22 + j, wall.at[shard_rows(near)], wall.at[shard_rows(near)], dev_par))
    for j in range(3):
        other = lax.rem(nw + 4 * (3 - j), 16)
        w_c.append(remote(25 + j, wall.at[shard_rows(other)], wall.at[shard_rows(other)], dev_par))

    w_z.start()
    far_a.start()
    far_b.start()
    up.start()
    down.start()
    par_mid.start()
    w_c[0].start()
    for copy in w_yn:
        copy.start()

    w_z.wait_recv()
    for copy in w_x:
        copy.start()
    up.wait_recv()
    par_bot.start()
    down.wait_recv()
    par_top.start()
    for copy in w_x:
        copy.wait_recv()
    w_c[1].start()
    for copy in w_yf:
        copy.start()

    par_mid.wait_recv()
    par_top.wait_recv()
    par_bot.wait_recv()
    load_q.wait()
    scale = 1.0 / math.sqrt(HD)
    far_there = jnp.where(c == 0, wa > 0, wa < N_WA - 1)

    def biases(r, head, beside, there):
        radius_row = win_ref[head, 0]
        radius_col = win_ref[head, 1]
        out = []
        for gap in (-1, 0, 1):
            row = T_ROWS * x + r + gap
            ok = (row >= 0) & (row < N_HA * T_ROWS) & (abs(gap) <= radius_row)
            if beside:
                ok = ok & (radius_col >= 1) & there
            out.append(jnp.where(ok, 0.0, MASKED).astype(jnp.float32))
        return out

    def lanes(head):
        return pl.ds(pl.multiple_of(head * HD, HD), HD)

    def token_rows(r, count):
        return pl.ds(pl.multiple_of(r * TOK, TOK), count * TOK)

    def query_tile(r, head):
        part = pl.ds(pl.multiple_of(r * HALF, HALF), HALF)
        return jnp.concatenate([qry[0, part, lanes(head)], qry[1, part, lanes(head)]], axis=0)

    def scores(query, buf, r, head, bias):
        keys = buf[0, token_rows(r, 3), lanes(head)]
        raw = lax.dot_general(query, keys, NT, preferred_element_type=jnp.float32) * scale
        return [raw[:, j * TOK : (j + 1) * TOK] + bias[j] for j in range(3)]

    def values(weights, buf, r, head):
        return jnp.dot(
            jnp.concatenate(weights, axis=1).astype(jnp.bfloat16),
            buf[1, token_rows(r, 3), lanes(head)],
            preferred_element_type=jnp.float32,
        )

    def total(parts, op):
        out = parts[0]
        for part in parts[1:]:
            out = op(out, part)
        return out

    def near_tile(index, carry):
        r = index // HEADS_HERE
        head = lax.rem(index, HEADS_HERE)
        query = query_tile(r, head)
        s_own = scores(query, own, r, head, biases(r, head, False, True))
        s_par = scores(query, par, r, head, biases(r, head, True, True))
        highest = jnp.max(total(s_own + s_par, jnp.maximum), axis=1, keepdims=True)
        p_own = [jnp.exp(s - highest) for s in s_own]
        p_par = [jnp.exp(s - highest) for s in s_par]
        norm = jnp.sum(total(p_own + p_par, jnp.add), axis=1, keepdims=True)
        o_part[index] = values(p_own, own, r, head) + values(p_par, par, r, head)
        m_part[index] = jnp.broadcast_to(highest, (TOK, HD))
        l_part[index] = jnp.broadcast_to(norm, (TOK, HD))
        return carry

    lax.fori_loop(0, T_ROWS * HEADS_HERE, near_tile, 0)

    far_a.wait_send()
    far_c.start()
    far_a.wait_recv()
    far_up.start()
    for j in range(3):
        w_yn[j].wait_recv()
        w_c[2 + j].start()
    far_b.wait_recv()
    far_down.start()
    for j in range(3):
        w_yf[j].wait_recv()
        w_c[5 + j].start()
    far_up.wait_recv()
    far_down.wait_recv()
    far_c.wait_recv()

    def far_tile(index, carry):
        r = index // HEADS_HERE
        head = lax.rem(index, HEADS_HERE)
        query = query_tile(r, head)
        s_far = scores(query, far, r, head, biases(r, head, True, far_there))
        before = m_part[index]
        highest = jnp.maximum(
            before, jnp.max(total(s_far, jnp.maximum), axis=1, keepdims=True)
        )
        shrink = jnp.exp(before - highest)
        p_far = [jnp.exp(s - highest) for s in s_far]
        norm = shrink * l_part[index] + jnp.sum(total(p_far, jnp.add), axis=1, keepdims=True)
        out = (shrink * o_part[index] + values(p_far, far, r, head)) / norm
        att[token_rows(r, 1), lanes(head)] = out.astype(jnp.bfloat16)
        return carry

    lax.fori_loop(0, T_ROWS * HEADS_HERE, far_tile, 0)
    for copy in w_c:
        copy.wait_recv()

    right = (x, wa, lax.rem(g + 1, N_TA))
    left = (x, wa, lax.rem(g + N_TA - 1, N_TA))

    def partial_sum(dest, r):
        weight = wall[pl.ds(pl.multiple_of(dest * FEAT, FEAT), FEAT), :]
        return lax.dot_general(
            att[token_rows(r, 1), :], weight, NT, preferred_element_type=jnp.float32
        )

    def hop_r(k):
        return pltpu.make_async_remote_copy(
            src_ref=slot_r.at[k],
            dst_ref=slot_r.at[k],
            send_sem=ssem_r.at[k],
            recv_sem=rsem_r.at[k],
            device_id=right,
            device_id_type=MESH,
        )

    def hop_l(k):
        return pltpu.make_async_remote_copy(
            src_ref=slot_l.at[k],
            dst_ref=slot_l.at[k],
            send_sem=ssem_l.at[k],
            recv_sem=rsem_l.at[k],
            device_id=left,
            device_id_type=MESH,
        )

    def hop(tau, carry):
        k = tau - 2 * g

        @pl.when((k >= 0) & (k < T_ROWS * (N_TA - 1 - g)))
        def _():
            @pl.when(g > 0)
            def _():
                hop_r(k).wait_recv()

            add = partial_sum(N_TA - 1 - k // T_ROWS, lax.rem(k, T_ROWS))
            slot_r[k] = (slot_r[k].astype(jnp.float32) + add).astype(jnp.bfloat16)
            hop_r(k).start()

        n = tau - 2 * (N_TA - 1 - g)

        @pl.when((n >= 0) & (n < T_ROWS * g))
        def _():
            @pl.when(g < N_TA - 1)
            def _():
                hop_l(n).wait_recv()

            add = partial_sum(n // T_ROWS, lax.rem(n, T_ROWS))
            slot_l[n] = (slot_l[n].astype(jnp.float32) + add).astype(jnp.bfloat16)
            hop_l(n).start()

        return carry

    lax.fori_loop(0, T_ROWS * (N_TA - 1), hop, 0)

    load_h.wait()
    load_m.wait()
    picked = mod[step_ref[0]]
    gate, shift, gain = picked[0:1], picked[1:2], picked[2:3]
    lane = lax.broadcasted_iota(jnp.int32, (TOK, HD), 1)
    for r in range(T_ROWS):
        own_part = partial_sum(g, r)
        k = T_ROWS * (N_TA - 1 - g) + r
        n = T_ROWS * g + r

        @pl.when(g > 0)
        def _():
            hop_r(k).wait_recv()

        @pl.when(g < N_TA - 1)
        def _():
            hop_l(n).wait_recv()

        projected = own_part + slot_r[k].astype(jnp.float32) + slot_l[n].astype(jnp.float32)
        part = pl.ds(r * HALF, HALF)
        before = jnp.concatenate([hid[0, part, :], hid[1, part, :]], axis=0).astype(jnp.float32)
        now = before + gate * projected
        mixed[pl.ds(r * TOK, TOK), :] = now
        rounded = now.astype(jnp.bfloat16)
        res_ref[0, part, :] = rounded[:HALF]
        res_ref[1, part, :] = rounded[HALF:]
        first = jnp.sum(now, axis=1, keepdims=True)
        second = jnp.sum(now * now, axis=1, keepdims=True)
        both = jnp.where(lane == 0, first, jnp.where(lane == 1, second, 0.0))
        stat[0, :, pl.ds(r * TOK, TOK)] = jnp.transpose(both)[:8]

    def share(j):
        return pltpu.make_async_remote_copy(
            src_ref=stat.at[0],
            dst_ref=stat.at[j + 1],
            send_sem=ssem_s.at[j],
            recv_sem=rsem_s.at[j],
            device_id=dev_t[j],
            device_id_type=MESH,
        )

    for j in range(7):
        share(j).start()
    for j in range(7):
        share(j).wait_recv()
    sums = total([stat[j] for j in range(N_TA)], jnp.add)
    for r in range(T_ROWS):
        line = sums[:, r * TOK : (r + 1) * TOK]
        column = jnp.transpose(jnp.concatenate([line] * (HD // 8), axis=0))
        average = column[:, 0:1] / D
        variance = column[:, 1:2] / D - average * average
        now = mixed[pl.ds(r * TOK, TOK), :]
        normed = (now - average) * lax.rsqrt(variance + EPSILON)
        out = (normed * (1.0 + gain) + shift).astype(jnp.bfloat16)
        part = pl.ds(r * HALF, HALF)
        ffn_ref[0, part, :] = out[:HALF]
        ffn_ref[1, part, :] = out[HALF:]

    for copy in [w_z, far_b, far_c, up, down, par_mid, par_top, par_bot, far_up, far_down]:
        copy.wait_send()
    for copy in w_x + w_yn + w_yf + w_c:
        copy.wait_send()
    for j in range(7):
        share(j).wait_send()

    def sent(k, carry):
        @pl.when(k < T_ROWS * (N_TA - 1 - g))
        def _():
            hop_r(k).wait_send()

        @pl.when(k < T_ROWS * g)
        def _():
            hop_l(k).wait_send()

        return carry

    lax.fori_loop(0, T_ROWS * (N_TA - 1), sent, 0)


def shards(hidden_states, queries, keys_values, out_weight, mod_table, windows, step_index):
    flat = (FRAMES, ROWS * COLS, FEAT)
    any_spec = pl.BlockSpec(memory_space=pl.ANY)
    smem_spec = pl.BlockSpec(memory_space=pltpu.SMEM)
    vmem_spec = pl.BlockSpec(memory_space=pltpu.VMEM)
    column = pltpu.VMEM((2, (T_ROWS + 2) * TOK, FEAT), jnp.bfloat16)
    tiles = T_ROWS * HEADS_HERE
    residual_out, ffn_input = pl.pallas_call(
        kernel,
        out_shape=[jax.ShapeDtypeStruct(flat, jnp.bfloat16)] * 2,
        in_specs=[smem_spec] * 2 + [any_spec] * 5,
        out_specs=[vmem_spec] * 2,
        scratch_shapes=[
            column,
            column,
            column,
            pltpu.VMEM((D, FEAT), jnp.bfloat16),
            pltpu.VMEM(flat, jnp.bfloat16),
            pltpu.VMEM(flat, jnp.bfloat16),
            pltpu.VMEM(mod_table.shape, jnp.float32),
            pltpu.VMEM((TOKENS, FEAT), jnp.bfloat16),
            pltpu.VMEM((tiles, TOK, HD), jnp.float32),
            pltpu.VMEM((tiles, TOK, HD), jnp.float32),
            pltpu.VMEM((tiles, TOK, HD), jnp.float32),
            pltpu.VMEM((N_PIECE, TOK, FEAT), jnp.bfloat16),
            pltpu.VMEM((N_PIECE, TOK, FEAT), jnp.bfloat16),
            pltpu.VMEM((TOKENS, FEAT), jnp.float32),
            pltpu.VMEM((N_TA, 8, TOKENS), jnp.float32),
            pltpu.SemaphoreType.DMA((10,)),
            pltpu.SemaphoreType.DMA((28,)),
            pltpu.SemaphoreType.DMA((28,)),
            pltpu.SemaphoreType.DMA((N_PIECE,)),
            pltpu.SemaphoreType.DMA((N_PIECE,)),
            pltpu.SemaphoreType.DMA((N_PIECE,)),
            pltpu.SemaphoreType.DMA((N_PIECE,)),
            pltpu.SemaphoreType.DMA((7,)),
            pltpu.SemaphoreType.DMA((7,)),
        ],
        compiler_params=pltpu.CompilerParams(
            collective_id=0, has_side_effects=True, vmem_limit_bytes=52 * 2**20
        ),
    )(
        windows,
        step_index,
        hidden_states.reshape(flat),
        queries.reshape(flat),
        keys_values.reshape((2,) + flat),
        out_weight.T,
        mod_table,
    )
    shape = (FRAMES, ROWS, COLS, FEAT)
    return residual_out.reshape(shape), ffn_input.reshape(shape)


def solution(mesh):
    return jax.shard_map(
        shards,
        mesh=mesh,
        in_specs=(
            P(None, "ha", "wa", "ta"),
            P(None, "ha", "wa", "ta"),
            P(None, None, "ha", "wa", "ta"),
            P("ta", "wa"),
            P(None, None, "ta"),
            P("ta", None),
            P(),
        ),
        out_specs=(P(None, "ha", "wa", "ta"), P(None, "ha", "wa", "ta")),
        check_vma=False,
    )
```

```python
import math

import jax
import jax.numpy as jnp
from jax import lax
from jax.experimental import pallas as pl
from jax.experimental.pallas import tpu as pltpu
from jax.sharding import PartitionSpec as P

D = 5120
HD = 128
TILE = 8
EPSILON = 1e-06

N_HA, N_WA, N_TA = 4, 16, 8
N_Y = 4
FRAMES, ROWS, COLS = 2, 24, 8
FEAT = 640
HEADS_HERE = 5
T_ROWS = ROWS // TILE
TOK = FRAMES * TILE * TILE
HALF = TILE * TILE
TOKENS = T_ROWS * TOK
SHARD = D // N_WA
QUARTER = SHARD // N_HA
N_PIECE = N_TA * T_ROWS
MASKED = -1e30
MESH = pl.DeviceIdType.MESH
NT = (((1,), (1,)), ((), ()))


def kernel(
    win_ref,
    step_ref,
    hid_ref,
    q_ref,
    kv_ref,
    wt_ref,
    mod_ref,
    res_ref,
    ffn_ref,
    own,
    par,
    far,
    wall,
    hid,
    qry,
    mod,
    att,
    o_part,
    m_part,
    l_part,
    slot_r,
    slot_l,
    mixed,
    stat,
    lsem,
    ssem,
    rsem,
    ssem_r,
    rsem_r,
    ssem_l,
    rsem_l,
    ssem_s,
    rsem_s,
):
    x = lax.axis_index("ha")
    wa = lax.axis_index("wa")
    g = lax.axis_index("ta")
    y = wa // 4
    zh = lax.rem(wa // 2, 2)
    c = lax.rem(wa, 2)
    nw = 4 * y + 2 * (1 - zh) + c

    dev_par = (x, 4 * y + 2 * zh + 1 - c, g)
    dev_far = (x, lax.rem(wa + 15 + 2 * c, 16), g)
    dev_z = (x, nw, g)
    dev_diag = (x, 4 * y + 2 * (1 - zh) + 1 - c, g)
    dev_via = (x, 15 * (wa // 8), g)
    dev_x = [(lax.rem(x + j + 1, N_HA), wa, g) for j in range(3)]
    dev_y = [(x, lax.rem(wa + 4 * (j + 1), 16), g) for j in range(3)]
    dev_t = [(x, wa, lax.rem(g + j + 1, N_TA)) for j in range(7)]

    def shard_rows(index):
        return pl.ds(pl.multiple_of(index * SHARD, SHARD), SHARD)

    def quarter_rows(index, part):
        return pl.ds(pl.multiple_of(index * SHARD + part * QUARTER, QUARTER), QUARTER)

    is_relay = (wa == 0) | (wa == N_WA - 1)
    has_far = (wa > 0) & (wa < N_WA - 1)
    is_via = (wa == 4) | (wa == 11)
    is_direct = has_far & (wa != 4) & (wa != 11)

    loads = []
    for f in range(FRAMES):
        for r in range(T_ROWS):
            loads.append(
                pltpu.make_async_copy(
                    kv_ref.at[:, f, pl.ds(r * HALF, HALF), :],
                    own.at[:, pl.ds((r + 1) * TOK + f * HALF, HALF), :],
                    lsem.at[f * T_ROWS + r],
                )
            )
    load_w = pltpu.make_async_copy(wt_ref, wall.at[shard_rows(wa)], lsem.at[6])
    load_q = pltpu.make_async_copy(q_ref, qry, lsem.at[7])
    load_h = pltpu.make_async_copy(hid_ref, hid, lsem.at[8])
    load_m = pltpu.make_async_copy(mod_ref, mod, lsem.at[9])
    for load in loads:
        load.start()
    load_w.start()
    load_q.start()
    load_h.start()
    load_m.start()

    @pl.when(is_relay)
    def _():
        far[...] = jnp.zeros_like(far)

    @pl.when(g == 0)
    def _():
        slot_r[...] = jnp.zeros_like(slot_r)

    @pl.when(g == N_TA - 1)
    def _():
        slot_l[...] = jnp.zeros_like(slot_l)

    barrier = pltpu.get_barrier_semaphore()
    peers = [dev_par, dev_far, dev_z, dev_diag] + dev_x + dev_y + dev_t
    for peer in peers:
        pl.semaphore_signal(barrier, inc=1, device_id=peer, device_id_type=MESH)
    for load in loads:
        load.wait()
    load_w.wait()
    pl.semaphore_wait(barrier, len(peers))

    def remote(index, src, dst, device):
        return pltpu.make_async_remote_copy(
            src_ref=src,
            dst_ref=dst,
            send_sem=ssem.at[index],
            recv_sem=rsem.at[index],
            device_id=device,
            device_id_type=MESH,
        )

    def rows(buf, first, count):
        return buf.at[:, pl.ds(first * TOK, count * TOK), :]

    w_z = remote(0, wall.at[quarter_rows(wa, x)], wall.at[quarter_rows(wa, x)], dev_z)
    far_a = remote(1, rows(own, 1, 1), rows(far, 1, 1), dev_far)
    def far_rows_b(src, device):
        return remote(2, rows(src, 3, 1), rows(far, 3, 1), device)

    def middle(buf, head):
        return buf.at[:, pl.ds(2 * TOK, TOK), pl.ds(head * HD, HD)]

    def far_head(head, src, device):
        return remote(28 + head, middle(src, head), middle(far, head), device)

    far_b = far_rows_b(own, dev_far)
    far_c = [far_head(head, own, dev_far) for head in range(HEADS_HERE)]
    passed = range(3, HEADS_HERE)
    up = remote(4, rows(own, 1, 1), rows(own, 4, 1), dev_x[2])
    down = remote(5, rows(own, 3, 1), rows(own, 0, 1), dev_x[0])
    par_mid = remote(6, rows(own, 1, 3), rows(par, 1, 3), dev_par)
    par_top = remote(7, rows(own, 0, 1), rows(par, 0, 1), dev_par)
    par_bot = remote(8, rows(own, 4, 1), rows(par, 4, 1), dev_par)
    far_up = remote(9, rows(far, 1, 1), rows(far, 4, 1), dev_x[2])
    far_down = remote(10, rows(far, 3, 1), rows(far, 0, 1), dev_x[0])
    w_x = [
        remote(11 + j, wall.at[quarter_rows(nw, x)], wall.at[quarter_rows(nw, x)], dev_x[j])
        for j in range(3)
    ]
    w_yn = [
        remote(14 + j, wall.at[shard_rows(wa)], wall.at[shard_rows(wa)], dev_y[j]) for j in range(3)
    ]
    w_yf = [
        remote(17 + j, wall.at[shard_rows(nw)], wall.at[shard_rows(nw)], dev_y[j]) for j in range(3)
    ]
    w_c = [
        remote(20, wall.at[shard_rows(wa)], wall.at[shard_rows(wa)], dev_par),
        remote(21, wall.at[shard_rows(nw)], wall.at[shard_rows(nw)], dev_par),
    ]
    for j in range(3):
        near = lax.rem(wa + 4 * (3 - j), 16)
        w_c.append(remote(22 + j, wall.at[shard_rows(near)], wall.at[shard_rows(near)], dev_par))
    for j in range(3):
        other = lax.rem(nw + 4 * (3 - j), 16)
        w_c.append(remote(25 + j, wall.at[shard_rows(other)], wall.at[shard_rows(other)], dev_par))

    w_z.start()

    @pl.when(has_far)
    def _():
        far_a.start()

    @pl.when(is_direct)
    def _():
        far_b.start()

    @pl.when(is_via)
    def _():
        far_rows_b(own, dev_via).start()
        for head in passed:
            far_head(head, own, dev_via).start()

    up.start()
    down.start()
    par_mid.start()
    w_c[0].start()
    for copy in w_yn:
        copy.start()

    w_z.wait_recv()
    for copy in w_x:
        copy.start()
    up.wait_recv()
    par_bot.start()
    down.wait_recv()
    par_top.start()
    for copy in w_x:
        copy.wait_recv()
    w_c[1].start()
    for copy in w_yf:
        copy.start()

    par_mid.wait_recv()
    par_top.wait_recv()
    par_bot.wait_recv()
    load_q.wait()

    @pl.when(is_relay)
    def _():
        far_b.wait_recv()
        far_rows_b(far, dev_diag).start()

    scale = 1.0 / math.sqrt(HD)
    far_there = jnp.where(c == 0, wa > 0, wa < N_WA - 1)

    def biases(r, head, beside, there):
        radius_row = win_ref[0, head]
        radius_col = win_ref[1, head]
        out = []
        for gap in (-1, 0, 1):
            row = T_ROWS * x + r + gap
            ok = (row >= 0) & (row < N_HA * T_ROWS) & (abs(gap) <= radius_row)
            if beside:
                ok = ok & (radius_col >= 1) & there
            out.append(jnp.where(ok, 0.0, MASKED).astype(jnp.float32))
        return out

    def lanes(head):
        return pl.ds(pl.multiple_of(head * HD, HD), HD)

    def token_rows(r, count):
        return pl.ds(r * TOK if isinstance(r, int) else pl.multiple_of(r * TOK, TOK), count * TOK)

    def query_tile(r, head):
        part = pl.ds(r * HALF if isinstance(r, int) else pl.multiple_of(r * HALF, HALF), HALF)
        return jnp.concatenate([qry[0, part, lanes(head)], qry[1, part, lanes(head)]], axis=0)

    def scores(query, buf, r, head, bias):
        keys = buf[0, token_rows(r, 3), lanes(head)]
        raw = lax.dot_general(query, keys, NT, preferred_element_type=jnp.float32) * scale
        return [raw[:, j * TOK : (j + 1) * TOK] + bias[j] for j in range(3)]

    def values(weights, buf, r, head):
        return jnp.dot(
            jnp.concatenate(weights, axis=1).astype(jnp.bfloat16),
            buf[1, token_rows(r, 3), lanes(head)],
            preferred_element_type=jnp.float32,
        )

    def total(parts, op):
        out = parts[0]
        for part in parts[1:]:
            out = op(out, part)
        return out

    def near_tile(index, carry):
        r = index // HEADS_HERE
        head = lax.rem(index, HEADS_HERE)
        query = query_tile(r, head)
        s_own = scores(query, own, r, head, biases(r, head, False, True))
        s_par = scores(query, par, r, head, biases(r, head, True, True))
        highest = jnp.max(total(s_own + s_par, jnp.maximum), axis=1, keepdims=True)
        p_own = [jnp.exp(s - highest) for s in s_own]
        p_par = [jnp.exp(s - highest) for s in s_par]
        norm = jnp.sum(total(p_own + p_par, jnp.add), axis=1, keepdims=True)
        o_part[index] = values(p_own, own, r, head) + values(p_par, par, r, head)
        m_part[index] = jnp.broadcast_to(highest, (TOK, HD))
        l_part[index] = jnp.broadcast_to(norm, (TOK, HD))
        return carry

    lax.fori_loop(0, T_ROWS * HEADS_HERE, near_tile, 0)

    @pl.when(has_far)
    def _():
        far_a.wait_send()
        for head in range(3):
            far_c[head].start()

    @pl.when(is_direct)
    def _():
        for head in passed:
            far_c[head].start()

    @pl.when(is_relay)
    def _():
        for head in passed:
            far_c[head].wait_recv()
            far_head(head, far, dev_diag).start()

    @pl.when(has_far)
    def _():
        far_a.wait_recv()
        far_up.start()

    for j in range(3):
        w_yn[j].wait_recv()
        w_c[2 + j].start()

    @pl.when(has_far)
    def _():
        far_b.wait_recv()
        far_down.start()

    for j in range(3):
        w_yf[j].wait_recv()
        w_c[5 + j].start()

    @pl.when(has_far)
    def _():
        far_up.wait_recv()
        far_down.wait_recv()

    def far_tile(r, head):
        index = r * HEADS_HERE + head
        query = query_tile(r, head)
        s_far = scores(query, far, r, head, biases(r, head, True, far_there))
        before = m_part[index]
        highest = jnp.maximum(
            before, jnp.max(total(s_far, jnp.maximum), axis=1, keepdims=True)
        )
        shrink = jnp.exp(before - highest)
        p_far = [jnp.exp(s - highest) for s in s_far]
        norm = shrink * l_part[index] + jnp.sum(total(p_far, jnp.add), axis=1, keepdims=True)
        out = (shrink * o_part[index] + values(p_far, far, r, head)) / norm
        att[token_rows(r, 1), lanes(head)] = out.astype(jnp.bfloat16)

    def far_step(head, carry):
        @pl.when(has_far)
        def _():
            pltpu.make_async_remote_copy(
                src_ref=middle(own, 0),
                dst_ref=middle(far, 0),
                send_sem=ssem.at[28 + head],
                recv_sem=rsem.at[28 + head],
                device_id=dev_far,
                device_id_type=MESH,
            ).wait_recv()

        for r in range(T_ROWS):
            far_tile(r, head)
        return carry

    lax.fori_loop(0, HEADS_HERE, far_step, 0)
    for copy in w_c:
        copy.wait_recv()

    right = (x, wa, lax.rem(g + 1, N_TA))
    left = (x, wa, lax.rem(g + N_TA - 1, N_TA))

    def partial_sum(dest, r):
        weight = wall[pl.ds(pl.multiple_of(dest * FEAT, FEAT), FEAT), :]
        return lax.dot_general(
            att[token_rows(r, 1), :], weight, NT, preferred_element_type=jnp.float32
        )

    def hop_r(k):
        return pltpu.make_async_remote_copy(
            src_ref=slot_r.at[k],
            dst_ref=slot_r.at[k],
            send_sem=ssem_r.at[k],
            recv_sem=rsem_r.at[k],
            device_id=right,
            device_id_type=MESH,
        )

    def hop_l(k):
        return pltpu.make_async_remote_copy(
            src_ref=slot_l.at[k],
            dst_ref=slot_l.at[k],
            send_sem=ssem_l.at[k],
            recv_sem=rsem_l.at[k],
            device_id=left,
            device_id_type=MESH,
        )

    def hop(tau, carry):
        k = tau - 2 * g

        @pl.when((k >= 0) & (k < T_ROWS * (N_TA - 1 - g)))
        def _():
            @pl.when(g > 0)
            def _():
                hop_r(k).wait_recv()

            add = partial_sum(N_TA - 1 - k // T_ROWS, lax.rem(k, T_ROWS))
            slot_r[k] = (slot_r[k].astype(jnp.float32) + add).astype(jnp.bfloat16)
            hop_r(k).start()

        n = tau - 2 * (N_TA - 1 - g)

        @pl.when((n >= 0) & (n < T_ROWS * g))
        def _():
            @pl.when(g < N_TA - 1)
            def _():
                hop_l(n).wait_recv()

            add = partial_sum(n // T_ROWS, lax.rem(n, T_ROWS))
            slot_l[n] = (slot_l[n].astype(jnp.float32) + add).astype(jnp.bfloat16)
            hop_l(n).start()

        return carry

    lax.fori_loop(0, T_ROWS * (N_TA - 1), hop, 0)

    load_h.wait()
    load_m.wait()
    gate, shift, gain = [mod[j, pl.ds(step_ref[0], 1), :] for j in range(3)]
    lane = lax.broadcasted_iota(jnp.int32, (TOK, HD), 1)

    def share(j, r):
        return pltpu.make_async_remote_copy(
            src_ref=stat.at[0, r],
            dst_ref=stat.at[j + 1, r],
            send_sem=ssem_s.at[j * T_ROWS + r],
            recv_sem=rsem_s.at[j * T_ROWS + r],
            device_id=dev_t[j],
            device_id_type=MESH,
        )

    for r in range(T_ROWS):
        own_part = partial_sum(g, r)
        k = T_ROWS * (N_TA - 1 - g) + r
        n = T_ROWS * g + r

        @pl.when(g > 0)
        def _():
            hop_r(k).wait_recv()

        @pl.when(g < N_TA - 1)
        def _():
            hop_l(n).wait_recv()

        projected = own_part + slot_r[k].astype(jnp.float32) + slot_l[n].astype(jnp.float32)
        part = pl.ds(r * HALF, HALF)
        before = jnp.concatenate([hid[0, part, :], hid[1, part, :]], axis=0).astype(jnp.float32)
        now = before + gate * projected
        mixed[pl.ds(r * TOK, TOK), :] = now
        rounded = now.astype(jnp.bfloat16)
        res_ref[0, part, :] = rounded[:HALF]
        res_ref[1, part, :] = rounded[HALF:]
        first = jnp.sum(now, axis=1, keepdims=True)
        second = jnp.sum(now * now, axis=1, keepdims=True)
        both = jnp.where(lane == 0, first, jnp.where(lane == 1, second, 0.0))
        stat[0, r] = jnp.transpose(both)[:8]
        for j in range(7):
            share(j, r).start()

    for r in range(T_ROWS):
        for j in range(7):
            share(j, r).wait_recv()
        line = total([stat[j, r] for j in range(N_TA)], jnp.add)
        column = jnp.transpose(jnp.concatenate([line] * (HD // 8), axis=0))
        average = column[:, 0:1] / D
        variance = column[:, 1:2] / D - average * average
        now = mixed[pl.ds(r * TOK, TOK), :]
        normed = (now - average) * lax.rsqrt(variance + EPSILON)
        out = (normed * (1.0 + gain) + shift).astype(jnp.bfloat16)
        part = pl.ds(r * HALF, HALF)
        ffn_ref[0, part, :] = out[:HALF]
        ffn_ref[1, part, :] = out[HALF:]

    for copy in [w_z, far_b, up, down, par_mid, par_top, par_bot]:
        copy.wait_send()
    for head in passed:
        far_c[head].wait_send()

    @pl.when(has_far)
    def _():
        for copy in [far_up, far_down] + far_c[:3]:
            copy.wait_send()

    for copy in w_x + w_yn + w_yf + w_c:
        copy.wait_send()
    for j in range(7):
        for r in range(T_ROWS):
            share(j, r).wait_send()

    def sent(k, carry):
        @pl.when(k < T_ROWS * (N_TA - 1 - g))
        def _():
            hop_r(k).wait_send()

        @pl.when(k < T_ROWS * g)
        def _():
            hop_l(k).wait_send()

        return carry

    lax.fori_loop(0, T_ROWS * (N_TA - 1), sent, 0)


def shards(hidden_states, queries, keys_values, out_weight, mod_table, windows, step_index):
    flat = (FRAMES, ROWS * COLS, FEAT)
    any_spec = pl.BlockSpec(memory_space=pl.ANY)
    smem_spec = pl.BlockSpec(memory_space=pltpu.SMEM)
    vmem_spec = pl.BlockSpec(memory_space=pltpu.VMEM)
    column = pltpu.VMEM((2, (T_ROWS + 2) * TOK, FEAT), jnp.bfloat16)
    tiles = T_ROWS * HEADS_HERE
    residual_out, ffn_input = pl.pallas_call(
        kernel,
        out_shape=[jax.ShapeDtypeStruct(flat, jnp.bfloat16)] * 2,
        in_specs=[smem_spec] * 2 + [any_spec] * 5,
        out_specs=[vmem_spec] * 2,
        scratch_shapes=[
            column,
            column,
            column,
            pltpu.VMEM((D, FEAT), jnp.bfloat16),
            pltpu.VMEM(flat, jnp.bfloat16),
            pltpu.VMEM(flat, jnp.bfloat16),
            pltpu.VMEM((3, mod_table.shape[0], FEAT), jnp.float32),
            pltpu.VMEM((TOKENS, FEAT), jnp.bfloat16),
            pltpu.VMEM((tiles, TOK, HD), jnp.float32),
            pltpu.VMEM((tiles, TOK, HD), jnp.float32),
            pltpu.VMEM((tiles, TOK, HD), jnp.float32),
            pltpu.VMEM((N_PIECE, TOK, FEAT), jnp.bfloat16),
            pltpu.VMEM((N_PIECE, TOK, FEAT), jnp.bfloat16),
            pltpu.VMEM((TOKENS, FEAT), jnp.float32),
            pltpu.VMEM((N_TA, T_ROWS, 8, HD), jnp.float32),
            pltpu.SemaphoreType.DMA((10,)),
            pltpu.SemaphoreType.DMA((33,)),
            pltpu.SemaphoreType.DMA((33,)),
            pltpu.SemaphoreType.DMA((N_PIECE,)),
            pltpu.SemaphoreType.DMA((N_PIECE,)),
            pltpu.SemaphoreType.DMA((N_PIECE,)),
            pltpu.SemaphoreType.DMA((N_PIECE,)),
            pltpu.SemaphoreType.DMA((7 * T_ROWS,)),
            pltpu.SemaphoreType.DMA((7 * T_ROWS,)),
        ],
        compiler_params=pltpu.CompilerParams(
            collective_id=0, has_side_effects=True, vmem_limit_bytes=52 * 2**20
        ),
    )(
        windows.T,
        step_index,
        hidden_states.reshape(flat),
        queries.reshape(flat),
        keys_values.reshape((2,) + flat),
        out_weight.T,
        mod_table.transpose(1, 0, 2),
    )
    shape = (FRAMES, ROWS, COLS, FEAT)
    return residual_out.reshape(shape), ffn_input.reshape(shape)


def solution(mesh):
    return jax.shard_map(
        shards,
        mesh=mesh,
        in_specs=(
            P(None, "ha", "wa", "ta"),
            P(None, "ha", "wa", "ta"),
            P(None, None, "ha", "wa", "ta"),
            P("ta", "wa"),
            P(None, None, "ta"),
            P("ta", None),
            P(),
        ),
        out_specs=(P(None, "ha", "wa", "ta"), P(None, "ha", "wa", "ta")),
        check_vma=False,
    )
```

```python
import math

import jax
import jax.numpy as jnp
from jax import lax
from jax.experimental import pallas as pl
from jax.experimental.pallas import tpu as pltpu
from jax.sharding import PartitionSpec as P

D = 5120
HD = 128
TILE = 8
EPSILON = 1e-06

N_HA, N_WA, N_TA = 4, 16, 8
N_Y = 4
FRAMES, ROWS, COLS = 2, 24, 8
FEAT = 640
HEADS_HERE = 5
T_ROWS = ROWS // TILE
TOK = FRAMES * TILE * TILE
HALF = TILE * TILE
TOKENS = T_ROWS * TOK
SHARD = D // N_WA
QUARTER = SHARD // N_HA
N_PIECE = N_TA * T_ROWS
MASKED = -1e30
MESH = pl.DeviceIdType.MESH
NT = (((1,), (1,)), ((), ()))


def kernel(
    win_ref,
    step_ref,
    hid_ref,
    q_ref,
    kv_ref,
    wt_ref,
    mod_ref,
    res_ref,
    ffn_ref,
    own,
    par,
    far,
    wall,
    hid,
    qry,
    mod,
    att,
    o_part,
    m_part,
    l_part,
    wext,
    slot_r,
    slot_l,
    mixed,
    stat,
    lsem,
    ssem,
    rsem,
    ssem_e,
    rsem_e,
    ssem_r,
    rsem_r,
    ssem_l,
    rsem_l,
    ssem_s,
    rsem_s,
):
    x = lax.axis_index("ha")
    wa = lax.axis_index("wa")
    g = lax.axis_index("ta")
    y = wa // 4
    zh = lax.rem(wa // 2, 2)
    c = lax.rem(wa, 2)
    nw = 4 * y + 2 * (1 - zh) + c

    dev_par = (x, 4 * y + 2 * zh + 1 - c, g)
    dev_far = (x, lax.rem(wa + 15 + 2 * c, 16), g)
    dev_z = (x, nw, g)
    dev_diag = (x, 4 * y + 2 * (1 - zh) + 1 - c, g)
    dev_via = (x, 15 * (wa // 8), g)
    dev_x = [(lax.rem(x + j + 1, N_HA), wa, g) for j in range(3)]
    dev_y = [(x, lax.rem(wa + 4 * (j + 1), 16), g) for j in range(3)]
    dev_t = [(x, wa, lax.rem(g + j + 1, N_TA)) for j in range(7)]

    is_end = (g == 0) | (g == N_TA - 1)
    is_next = (g == 1) | (g == N_TA - 2)
    upper = g // (N_TA // 2)
    ext_y = (N_Y - 1) * (1 - upper)
    dev_next = (x, wa, 1 + (N_TA - 3) * upper)

    def shard_rows(index):
        return pl.ds(pl.multiple_of(index * SHARD, SHARD), SHARD)

    def quarter_rows(index, part):
        return pl.ds(pl.multiple_of(index * SHARD + part * QUARTER, QUARTER), QUARTER)

    is_relay = (wa == 0) | (wa == N_WA - 1)
    has_far = (wa > 0) & (wa < N_WA - 1)
    is_via = (wa == 4) | (wa == 11)
    is_direct = has_far & (wa != 4) & (wa != 11)

    loads = []
    for f in range(FRAMES):
        for r in range(T_ROWS):
            loads.append(
                pltpu.make_async_copy(
                    kv_ref.at[:, f, pl.ds(r * HALF, HALF), :],
                    own.at[:, pl.ds((r + 1) * TOK + f * HALF, HALF), :],
                    lsem.at[f * T_ROWS + r],
                )
            )
    load_w = pltpu.make_async_copy(wt_ref, wall.at[shard_rows(wa)], lsem.at[6])
    load_q = pltpu.make_async_copy(q_ref, qry, lsem.at[7])
    load_h = pltpu.make_async_copy(hid_ref, hid, lsem.at[8])
    load_m = pltpu.make_async_copy(mod_ref, mod, lsem.at[9])
    for load in loads:
        load.start()
    load_w.start()
    load_q.start()
    load_h.start()
    load_m.start()

    @pl.when(is_relay)
    def _():
        far[...] = jnp.zeros_like(far)

    @pl.when(g == 0)
    def _():
        slot_r[N_PIECE - T_ROWS :] = jnp.zeros((T_ROWS, TOK, FEAT), jnp.bfloat16)

    @pl.when(g == N_TA - 1)
    def _():
        slot_l[N_PIECE - T_ROWS :] = jnp.zeros((T_ROWS, TOK, FEAT), jnp.bfloat16)

    barrier = pltpu.get_barrier_semaphore()
    peers = [dev_par, dev_far, dev_z, dev_diag] + dev_x + dev_y + dev_t
    for peer in peers:
        pl.semaphore_signal(barrier, inc=1, device_id=peer, device_id_type=MESH)
    for load in loads:
        load.wait()
    load_w.wait()
    pl.semaphore_wait(barrier, len(peers))

    def remote(index, src, dst, device):
        return pltpu.make_async_remote_copy(
            src_ref=src,
            dst_ref=dst,
            send_sem=ssem.at[index],
            recv_sem=rsem.at[index],
            device_id=device,
            device_id_type=MESH,
        )

    def rows(buf, first, count):
        return buf.at[:, pl.ds(first * TOK, count * TOK), :]

    w_z = remote(0, wall.at[quarter_rows(wa, x)], wall.at[quarter_rows(wa, x)], dev_z)
    far_a = remote(1, rows(own, 1, 1), rows(far, 1, 1), dev_far)
    def far_rows_b(src, device):
        return remote(2, rows(src, 3, 1), rows(far, 3, 1), device)

    def middle(buf, head):
        return buf.at[:, pl.ds(2 * TOK, TOK), pl.ds(head * HD, HD)]

    def far_head(head, src, device):
        return remote(28 + head, middle(src, head), middle(far, head), device)

    far_b = far_rows_b(own, dev_far)
    far_c = [far_head(head, own, dev_far) for head in range(HEADS_HERE)]
    passed = range(3, HEADS_HERE)
    up = remote(4, rows(own, 1, 1), rows(own, 4, 1), dev_x[2])
    down = remote(5, rows(own, 3, 1), rows(own, 0, 1), dev_x[0])
    par_mid = remote(6, rows(own, 1, 3), rows(par, 1, 3), dev_par)
    par_top = remote(7, rows(own, 0, 1), rows(par, 0, 1), dev_par)
    par_bot = remote(8, rows(own, 4, 1), rows(par, 4, 1), dev_par)
    far_up = remote(9, rows(far, 1, 1), rows(far, 4, 1), dev_x[2])
    far_down = remote(10, rows(far, 3, 1), rows(far, 0, 1), dev_x[0])
    w_x = [
        remote(11 + j, wall.at[quarter_rows(nw, x)], wall.at[quarter_rows(nw, x)], dev_x[j])
        for j in range(3)
    ]
    w_yn = [
        remote(14 + j, wall.at[shard_rows(wa)], wall.at[shard_rows(wa)], dev_y[j]) for j in range(3)
    ]
    w_yf = [
        remote(17 + j, wall.at[shard_rows(nw)], wall.at[shard_rows(nw)], dev_y[j]) for j in range(3)
    ]
    w_c = [
        remote(20, wall.at[shard_rows(wa)], wall.at[shard_rows(wa)], dev_par),
        remote(21, wall.at[shard_rows(nw)], wall.at[shard_rows(nw)], dev_par),
    ]
    for j in range(3):
        near = lax.rem(wa + 4 * (3 - j), 16)
        w_c.append(remote(22 + j, wall.at[shard_rows(near)], wall.at[shard_rows(near)], dev_par))
    for j in range(3):
        other = lax.rem(nw + 4 * (3 - j), 16)
        w_c.append(remote(25 + j, wall.at[shard_rows(other)], wall.at[shard_rows(other)], dev_par))

    def ext_quarter(half, part):
        return wext.at[pl.ds(pl.multiple_of((2 * half + c) * SHARD + part * QUARTER, QUARTER), QUARTER)]

    def ext_shard(half):
        return wext.at[pl.ds(pl.multiple_of((2 * half + c) * SHARD, SHARD), SHARD)]

    def ext(send, recv, src, dst, device):
        return pltpu.make_async_remote_copy(
            src_ref=src,
            dst_ref=dst,
            send_sem=ssem_e.at[send],
            recv_sem=rsem_e.at[recv],
            device_id=device,
            device_id_type=MESH,
        )

    ext_t = ext(0, 0, wall.at[quarter_rows(wa, x)], ext_quarter(zh, x), dev_next)
    ext_z = ext(0, 1, ext_quarter(zh, x), ext_quarter(zh, x), dev_z)
    ext_y_copies = [
        ext(1 + 2 * j + n, n, ext_quarter(half, x), ext_quarter(half, x), dev_y[j])
        for j in range(3)
        for n, half in ((0, zh), (1, 1 - zh))
    ]
    ext_x_copies = [
        ext(7 + 2 * j + n, 2 + 2 * j + n, ext_quarter(half, x), ext_quarter(half, x), dev_x[j])
        for j in range(3)
        for n, half in ((0, zh), (1, 1 - zh))
    ]
    ext_c_copies = [
        ext(13 + n, 8 + n, ext_shard(half), ext_shard(half), dev_par)
        for n, half in ((0, zh), (1, 1 - zh))
    ]

    w_z.start()

    @pl.when(is_end & (y == ext_y))
    def _():
        ext_t.start()

    @pl.when(has_far)
    def _():
        far_a.start()

    @pl.when(is_direct)
    def _():
        far_b.start()

    @pl.when(is_via)
    def _():
        far_rows_b(own, dev_via).start()
        for head in passed:
            far_head(head, own, dev_via).start()

    up.start()
    down.start()
    par_mid.start()
    w_c[0].start()
    for copy in w_yn:
        copy.start()

    w_z.wait_recv()
    for copy in w_x:
        copy.start()
    up.wait_recv()
    par_bot.start()
    down.wait_recv()
    par_top.start()
    for copy in w_x:
        copy.wait_recv()
    w_c[1].start()
    for copy in w_yf:
        copy.start()

    par_mid.wait_recv()
    par_top.wait_recv()
    par_bot.wait_recv()
    load_q.wait()

    @pl.when(is_relay)
    def _():
        far_b.wait_recv()
        far_rows_b(far, dev_diag).start()


    @pl.when(is_next & (y == ext_y))
    def _():
        ext_t.wait_recv()
        ext_z.start()

    scale = 1.0 / math.sqrt(HD)
    far_there = jnp.where(c == 0, wa > 0, wa < N_WA - 1)

    def biases(r, head, beside, there):
        radius_row = win_ref[0, head]
        radius_col = win_ref[1, head]
        out = []
        for gap in (-1, 0, 1):
            row = T_ROWS * x + r + gap
            ok = (row >= 0) & (row < N_HA * T_ROWS) & (abs(gap) <= radius_row)
            if beside:
                ok = ok & (radius_col >= 1) & there
            out.append(jnp.where(ok, 0.0, MASKED).astype(jnp.float32))
        return out

    def lanes(head):
        return pl.ds(pl.multiple_of(head * HD, HD), HD)

    def token_rows(r, count):
        return pl.ds(r * TOK if isinstance(r, int) else pl.multiple_of(r * TOK, TOK), count * TOK)

    def query_tile(r, head):
        part = pl.ds(r * HALF if isinstance(r, int) else pl.multiple_of(r * HALF, HALF), HALF)
        return jnp.concatenate([qry[0, part, lanes(head)], qry[1, part, lanes(head)]], axis=0)

    def scores(query, buf, r, head, bias):
        keys = buf[0, token_rows(r, 3), lanes(head)]
        raw = lax.dot_general(query, keys, NT, preferred_element_type=jnp.float32) * scale
        return [raw[:, j * TOK : (j + 1) * TOK] + bias[j] for j in range(3)]

    def values(weights, buf, r, head):
        return jnp.dot(
            jnp.concatenate(weights, axis=1).astype(jnp.bfloat16),
            buf[1, token_rows(r, 3), lanes(head)],
            preferred_element_type=jnp.float32,
        )

    def total(parts, op):
        out = parts[0]
        for part in parts[1:]:
            out = op(out, part)
        return out

    def near_tile(index, carry):
        r = index // HEADS_HERE
        head = lax.rem(index, HEADS_HERE)
        query = query_tile(r, head)
        s_own = scores(query, own, r, head, biases(r, head, False, True))
        s_par = scores(query, par, r, head, biases(r, head, True, True))
        highest = jnp.max(total(s_own + s_par, jnp.maximum), axis=1, keepdims=True)
        p_own = [jnp.exp(s - highest) for s in s_own]
        p_par = [jnp.exp(s - highest) for s in s_par]
        norm = jnp.sum(total(p_own + p_par, jnp.add), axis=1, keepdims=True)
        o_part[index] = values(p_own, own, r, head) + values(p_par, par, r, head)
        m_part[index] = jnp.broadcast_to(highest, (TOK, HD))
        l_part[index] = jnp.broadcast_to(norm, (TOK, HD))
        return carry

    lax.fori_loop(0, T_ROWS * HEADS_HERE, near_tile, 0)

    @pl.when(has_far)
    def _():
        far_a.wait_send()
        for head in range(3):
            far_c[head].start()

    @pl.when(is_direct)
    def _():
        for head in passed:
            far_c[head].start()

    @pl.when(is_relay)
    def _():
        for head in passed:
            far_c[head].wait_recv()
            far_head(head, far, dev_diag).start()

    @pl.when(is_next & (y == ext_y))
    def _():
        ext_z.wait_recv()
        for copy in ext_y_copies:
            copy.start()

    @pl.when(has_far)
    def _():
        far_a.wait_recv()
        far_up.start()

    for j in range(3):
        w_yn[j].wait_recv()
        w_c[2 + j].start()

    @pl.when(is_next)
    def _():
        @pl.when(y != ext_y)
        def _():
            for copy in ext_y_copies[:2]:
                copy.wait_recv()

        for copy in ext_x_copies:
            copy.start()

    @pl.when(has_far)
    def _():
        far_b.wait_recv()
        far_down.start()

    for j in range(3):
        w_yf[j].wait_recv()
        w_c[5 + j].start()

    @pl.when(is_next)
    def _():
        for copy in ext_x_copies:
            copy.wait_recv()
        for copy in ext_c_copies:
            copy.start()

    @pl.when(has_far)
    def _():
        far_up.wait_recv()
        far_down.wait_recv()

    def far_tile(r, head):
        index = r * HEADS_HERE + head
        query = query_tile(r, head)
        s_far = scores(query, far, r, head, biases(r, head, True, far_there))
        before = m_part[index]
        highest = jnp.maximum(
            before, jnp.max(total(s_far, jnp.maximum), axis=1, keepdims=True)
        )
        shrink = jnp.exp(before - highest)
        p_far = [jnp.exp(s - highest) for s in s_far]
        norm = shrink * l_part[index] + jnp.sum(total(p_far, jnp.add), axis=1, keepdims=True)
        out = (shrink * o_part[index] + values(p_far, far, r, head)) / norm
        att[token_rows(r, 1), lanes(head)] = out.astype(jnp.bfloat16)

    def far_step(head, carry):
        @pl.when(has_far)
        def _():
            pltpu.make_async_remote_copy(
                src_ref=middle(own, 0),
                dst_ref=middle(far, 0),
                send_sem=ssem.at[28 + head],
                recv_sem=rsem.at[28 + head],
                device_id=dev_far,
                device_id_type=MESH,
            ).wait_recv()

        for r in range(T_ROWS):
            far_tile(r, head)
        return carry

    lax.fori_loop(0, HEADS_HERE, far_step, 0)
    for copy in w_c:
        copy.wait_recv()

    @pl.when(is_next)
    def _():
        for copy in ext_c_copies:
            copy.wait_recv()

    right = (x, wa, lax.rem(g + 1, N_TA))
    left = (x, wa, lax.rem(g + N_TA - 1, N_TA))

    def partial_sum(dest, r):
        weight = wall[pl.ds(pl.multiple_of(dest * FEAT, FEAT), FEAT), :]
        return lax.dot_general(
            att[token_rows(r, 1), :], weight, NT, preferred_element_type=jnp.float32
        )

    def extra_sum(taken, far_dest):
        weight = wext[pl.ds(pl.multiple_of(far_dest * FEAT, FEAT), FEAT), :]
        return lax.dot_general(taken, weight, NT, preferred_element_type=jnp.float32)

    def flow(slots, send, recv, device):
        def hop(src, k):
            return pltpu.make_async_remote_copy(
                src_ref=src,
                dst_ref=slots.at[k],
                send_sem=send.at[k],
                recv_sem=recv.at[k],
                device_id=device,
                device_id_type=MESH,
            )

        return hop

    hop_r = flow(slot_r, ssem_r, rsem_r, right)
    hop_l = flow(slot_l, ssem_l, rsem_l, left)

    def step(hop, slots, k, place, dest_of, ext_of):
        r = lax.rem(k, T_ROWS)
        taken = 2 * T_ROWS

        @pl.when((place == 0) & (k < T_ROWS))
        def _():
            hop(att.at[token_rows(r, 1)], k).start()

        @pl.when((place == 0) & (k >= taken))
        def _():
            slots[k] = partial_sum(dest_of(k), r).astype(jnp.bfloat16)
            hop(slots.at[k], k).start()

        @pl.when((place == 1) & (k < T_ROWS))
        def _():
            hop(slots.at[k], k).wait_recv()
            add = partial_sum(dest_of(k), r) + extra_sum(slots[k], ext_of(k))
            slots[N_PIECE - T_ROWS + r] = add.astype(jnp.bfloat16)
            hop(slots.at[N_PIECE - T_ROWS + r], k).start()

        @pl.when((place == 1) & (k >= T_ROWS) & (k < taken))
        def _():
            add = partial_sum(dest_of(k), r) + extra_sum(slots[r], ext_of(k))
            slots[k] = add.astype(jnp.bfloat16)
            hop(slots.at[k], k).start()

        @pl.when((place > 1) | ((place == 1) & (k >= taken)))
        def _():
            hop(slots.at[k], k).wait_recv()
            add = partial_sum(dest_of(k), r)
            slots[k] = (slots[k].astype(jnp.float32) + add).astype(jnp.bfloat16)
            hop(slots.at[k], k).start()

    def hops(tau, carry):
        k = tau - 2 * g

        @pl.when((k >= 0) & (k < T_ROWS * (N_TA - 1 - g)))
        def _():
            step(
                hop_r, slot_r, k, g, lambda m: N_TA - 1 - m // T_ROWS, lambda m: 1 - m // T_ROWS
            )

        n = tau - 2 * (N_TA - 1 - g)

        @pl.when((n >= 0) & (n < T_ROWS * g))
        def _():
            step(hop_l, slot_l, n, N_TA - 1 - g, lambda m: m // T_ROWS, lambda m: m // T_ROWS)

        return carry

    lax.fori_loop(0, T_ROWS * (N_TA - 1), hops, 0)

    load_h.wait()
    load_m.wait()
    gate, shift, gain = [mod[j, pl.ds(step_ref[0], 1), :] for j in range(3)]
    lane = lax.broadcasted_iota(jnp.int32, (TOK, HD), 1)

    def share(j, r):
        return pltpu.make_async_remote_copy(
            src_ref=stat.at[0, r],
            dst_ref=stat.at[j + 1, r],
            send_sem=ssem_s.at[j * T_ROWS + r],
            recv_sem=rsem_s.at[j * T_ROWS + r],
            device_id=dev_t[j],
            device_id_type=MESH,
        )

    for r in range(T_ROWS):
        own_part = partial_sum(g, r)
        k = T_ROWS * (N_TA - 1 - g) + r
        n = T_ROWS * g + r

        @pl.when(g > 0)
        def _():
            hop_r(slot_r.at[k], k).wait_recv()

        @pl.when(g < N_TA - 1)
        def _():
            hop_l(slot_l.at[n], n).wait_recv()

        projected = own_part + slot_r[k].astype(jnp.float32) + slot_l[n].astype(jnp.float32)
        part = pl.ds(r * HALF, HALF)
        before = jnp.concatenate([hid[0, part, :], hid[1, part, :]], axis=0).astype(jnp.float32)
        now = before + gate * projected
        mixed[pl.ds(r * TOK, TOK), :] = now
        rounded = now.astype(jnp.bfloat16)
        res_ref[0, part, :] = rounded[:HALF]
        res_ref[1, part, :] = rounded[HALF:]
        first = jnp.sum(now, axis=1, keepdims=True)
        second = jnp.sum(now * now, axis=1, keepdims=True)
        both = jnp.where(lane == 0, first, jnp.where(lane == 1, second, 0.0))
        stat[0, r] = jnp.transpose(both)[:8]
        for j in range(7):
            share(j, r).start()

    for r in range(T_ROWS):
        for j in range(7):
            share(j, r).wait_recv()
        line = total([stat[j, r] for j in range(N_TA)], jnp.add)
        column = jnp.transpose(jnp.concatenate([line] * (HD // 8), axis=0))
        average = column[:, 0:1] / D
        variance = column[:, 1:2] / D - average * average
        now = mixed[pl.ds(r * TOK, TOK), :]
        normed = (now - average) * lax.rsqrt(variance + EPSILON)
        out = (normed * (1.0 + gain) + shift).astype(jnp.bfloat16)
        part = pl.ds(r * HALF, HALF)
        ffn_ref[0, part, :] = out[:HALF]
        ffn_ref[1, part, :] = out[HALF:]

    for copy in [w_z, far_b, up, down, par_mid, par_top, par_bot]:
        copy.wait_send()
    for head in passed:
        far_c[head].wait_send()

    @pl.when(has_far)
    def _():
        for copy in [far_up, far_down] + far_c[:3]:
            copy.wait_send()

    for copy in w_x + w_yn + w_yf + w_c:
        copy.wait_send()
    for j in range(7):
        for r in range(T_ROWS):
            share(j, r).wait_send()

    @pl.when(is_end & (y == ext_y))
    def _():
        ext_t.wait_send()

    @pl.when(is_next)
    def _():
        @pl.when(y == ext_y)
        def _():
            for copy in [ext_z] + ext_y_copies:
                copy.wait_send()

        for copy in ext_x_copies + ext_c_copies:
            copy.wait_send()

    def sent(k, carry):
        left_out = (k >= T_ROWS) & (k < 2 * T_ROWS)

        @pl.when((k < T_ROWS * (N_TA - 1 - g)) & ~((g == 0) & left_out))
        def _():
            hop_r(slot_r.at[k], k).wait_send()

        @pl.when((k < T_ROWS * g) & ~((g == N_TA - 1) & left_out))
        def _():
            hop_l(slot_l.at[k], k).wait_send()

        return carry

    lax.fori_loop(0, T_ROWS * (N_TA - 1), sent, 0)


def shards(hidden_states, queries, keys_values, out_weight, mod_table, windows, step_index):
    flat = (FRAMES, ROWS * COLS, FEAT)
    any_spec = pl.BlockSpec(memory_space=pl.ANY)
    smem_spec = pl.BlockSpec(memory_space=pltpu.SMEM)
    vmem_spec = pl.BlockSpec(memory_space=pltpu.VMEM)
    column = pltpu.VMEM((2, (T_ROWS + 2) * TOK, FEAT), jnp.bfloat16)
    tiles = T_ROWS * HEADS_HERE
    residual_out, ffn_input = pl.pallas_call(
        kernel,
        out_shape=[jax.ShapeDtypeStruct(flat, jnp.bfloat16)] * 2,
        in_specs=[smem_spec] * 2 + [any_spec] * 5,
        out_specs=[vmem_spec] * 2,
        scratch_shapes=[
            column,
            column,
            column,
            pltpu.VMEM((D, FEAT), jnp.bfloat16),
            pltpu.VMEM(flat, jnp.bfloat16),
            pltpu.VMEM(flat, jnp.bfloat16),
            pltpu.VMEM((3, mod_table.shape[0], FEAT), jnp.float32),
            pltpu.VMEM((TOKENS, FEAT), jnp.bfloat16),
            pltpu.VMEM((tiles, TOK, HD), jnp.float32),
            pltpu.VMEM((tiles, TOK, HD), jnp.float32),
            pltpu.VMEM((tiles, TOK, HD), jnp.float32),
            pltpu.VMEM((4 * SHARD, FEAT), jnp.bfloat16),
            pltpu.VMEM((N_PIECE, TOK, FEAT), jnp.bfloat16),
            pltpu.VMEM((N_PIECE, TOK, FEAT), jnp.bfloat16),
            pltpu.VMEM((TOKENS, FEAT), jnp.float32),
            pltpu.VMEM((N_TA, T_ROWS, 8, HD), jnp.float32),
            pltpu.SemaphoreType.DMA((10,)),
            pltpu.SemaphoreType.DMA((33,)),
            pltpu.SemaphoreType.DMA((33,)),
            pltpu.SemaphoreType.DMA((15,)),
            pltpu.SemaphoreType.DMA((10,)),
            pltpu.SemaphoreType.DMA((N_PIECE,)),
            pltpu.SemaphoreType.DMA((N_PIECE,)),
            pltpu.SemaphoreType.DMA((N_PIECE,)),
            pltpu.SemaphoreType.DMA((N_PIECE,)),
            pltpu.SemaphoreType.DMA((7 * T_ROWS,)),
            pltpu.SemaphoreType.DMA((7 * T_ROWS,)),
        ],
        compiler_params=pltpu.CompilerParams(
            collective_id=0, has_side_effects=True, vmem_limit_bytes=60 * 2**20
        ),
    )(
        windows.T,
        step_index,
        hidden_states.reshape(flat),
        queries.reshape(flat),
        keys_values.reshape((2,) + flat),
        out_weight.T,
        mod_table.transpose(1, 0, 2),
    )
    shape = (FRAMES, ROWS, COLS, FEAT)
    return residual_out.reshape(shape), ffn_input.reshape(shape)


def solution(mesh):
    return jax.shard_map(
        shards,
        mesh=mesh,
        in_specs=(
            P(None, "ha", "wa", "ta"),
            P(None, "ha", "wa", "ta"),
            P(None, None, "ha", "wa", "ta"),
            P("ta", "wa"),
            P(None, None, "ta"),
            P("ta", None),
            P(),
        ),
        out_specs=(P(None, "ha", "wa", "ta"), P(None, "ha", "wa", "ta")),
        check_vma=False,
    )
```

```python
import math

import jax
import jax.numpy as jnp
from jax import lax
from jax.experimental import pallas as pl
from jax.experimental.pallas import tpu as pltpu
from jax.sharding import PartitionSpec as P

D = 5120
HD = 128
TILE = 8
EPSILON = 1e-06

N_HA, N_WA, N_TA = 4, 16, 8
N_Y = 4
FRAMES, ROWS, COLS = 2, 24, 8
FEAT = 640
HEADS_HERE = 5
T_ROWS = ROWS // TILE
TOK = FRAMES * TILE * TILE
HALF = TILE * TILE
TOKENS = T_ROWS * TOK
SHARD = D // N_WA
QUARTER = SHARD // N_HA
N_PIECE = N_TA * T_ROWS
MASKED = -1e30
MESH = pl.DeviceIdType.MESH
NT = (((1,), (1,)), ((), ()))


def kernel(
    win_ref,
    step_ref,
    hid_ref,
    q_ref,
    kv_ref,
    wt_ref,
    mod_ref,
    res_ref,
    ffn_ref,
    own,
    par,
    far,
    wall,
    hid,
    qry,
    mod,
    att,
    o_part,
    m_part,
    l_part,
    wext,
    slot_r,
    slot_l,
    mixed,
    stat,
    lsem,
    ssem,
    rsem,
    ssem_e,
    rsem_e,
    ssem_r,
    rsem_r,
    ssem_l,
    rsem_l,
    ssem_s,
    rsem_s,
):
    x = lax.axis_index("ha")
    wa = lax.axis_index("wa")
    g = lax.axis_index("ta")
    y = wa // 4
    zh = lax.rem(wa // 2, 2)
    c = lax.rem(wa, 2)
    nw = 4 * y + 2 * (1 - zh) + c

    dev_par = (x, 4 * y + 2 * zh + 1 - c, g)
    dev_far = (x, lax.rem(wa + 15 + 2 * c, 16), g)
    dev_z = (x, nw, g)
    dev_diag = (x, 4 * y + 2 * (1 - zh) + 1 - c, g)
    dev_via = (x, 15 * (wa // 8), g)
    dev_x = [(lax.rem(x + j + 1, N_HA), wa, g) for j in range(3)]
    dev_y = [(x, lax.rem(wa + 4 * (j + 1), 16), g) for j in range(3)]
    dev_t = [(x, wa, lax.rem(g + j + 1, N_TA)) for j in range(7)]

    is_end = (g == 0) | (g == N_TA - 1)
    is_next = (g == 1) | (g == N_TA - 2)
    upper = g // (N_TA // 2)
    ext_y = (N_Y - 1) * (1 - upper)
    dev_next = (x, wa, 1 + (N_TA - 3) * upper)
    dev_cross = (x, nw, 1 + (N_TA - 3) * upper)
    dev_beside = (x, nw, g + 1 - 2 * lax.rem(g, 2))

    def shard_rows(index):
        return pl.ds(pl.multiple_of(index * SHARD, SHARD), SHARD)

    def quarter_rows(index, part):
        return pl.ds(pl.multiple_of(index * SHARD + part * QUARTER, QUARTER), QUARTER)

    is_relay = (wa == 0) | (wa == N_WA - 1)
    has_far = (wa > 0) & (wa < N_WA - 1)
    is_via = (wa == 4) | (wa == 11)
    is_direct = has_far & (wa != 4) & (wa != 11)

    loads = []
    for f in range(FRAMES):
        for r in range(T_ROWS):
            loads.append(
                pltpu.make_async_copy(
                    kv_ref.at[:, f, pl.ds(r * HALF, HALF), :],
                    own.at[:, pl.ds((r + 1) * TOK + f * HALF, HALF), :],
                    lsem.at[f * T_ROWS + r],
                )
            )
    load_w = pltpu.make_async_copy(wt_ref, wall.at[shard_rows(wa)], lsem.at[6])
    load_q = pltpu.make_async_copy(q_ref, qry, lsem.at[7])
    load_h = pltpu.make_async_copy(hid_ref, hid, lsem.at[8])
    load_m = pltpu.make_async_copy(mod_ref, mod, lsem.at[9])
    for load in loads:
        load.start()
    load_w.start()
    load_q.start()
    load_h.start()
    load_m.start()

    @pl.when(is_relay)
    def _():
        far[...] = jnp.zeros_like(far)

    @pl.when(g == 0)
    def _():
        slot_r[N_PIECE - T_ROWS :] = jnp.zeros((T_ROWS, TOK, FEAT), jnp.bfloat16)

    @pl.when(g == N_TA - 1)
    def _():
        slot_l[N_PIECE - T_ROWS :] = jnp.zeros((T_ROWS, TOK, FEAT), jnp.bfloat16)

    barrier = pltpu.get_barrier_semaphore()
    peers = [dev_par, dev_far, dev_z, dev_diag, dev_beside] + dev_x + dev_y + dev_t
    for peer in peers:
        pl.semaphore_signal(barrier, inc=1, device_id=peer, device_id_type=MESH)
    for load in loads:
        load.wait()
    load_w.wait()
    pl.semaphore_wait(barrier, len(peers))

    def remote(index, src, dst, device):
        return pltpu.make_async_remote_copy(
            src_ref=src,
            dst_ref=dst,
            send_sem=ssem.at[index],
            recv_sem=rsem.at[index],
            device_id=device,
            device_id_type=MESH,
        )

    def rows(buf, first, count):
        return buf.at[:, pl.ds(first * TOK, count * TOK), :]

    w_z = remote(0, wall.at[quarter_rows(wa, x)], wall.at[quarter_rows(wa, x)], dev_z)
    far_a = remote(1, rows(own, 1, 1), rows(far, 1, 1), dev_far)
    def far_rows_b(src, device):
        return remote(2, rows(src, 3, 1), rows(far, 3, 1), device)

    def middle(buf, head):
        return buf.at[:, pl.ds(2 * TOK, TOK), pl.ds(head * HD, HD)]

    def far_head(head, src, device):
        return remote(28 + head, middle(src, head), middle(far, head), device)

    far_b = far_rows_b(own, dev_far)
    far_c = [far_head(head, own, dev_far) for head in range(HEADS_HERE)]
    passed = range(3, HEADS_HERE)
    up = remote(4, rows(own, 1, 1), rows(own, 4, 1), dev_x[2])
    down = remote(5, rows(own, 3, 1), rows(own, 0, 1), dev_x[0])
    par_mid = remote(6, rows(own, 1, 3), rows(par, 1, 3), dev_par)
    par_top = remote(7, rows(own, 0, 1), rows(par, 0, 1), dev_par)
    par_bot = remote(8, rows(own, 4, 1), rows(par, 4, 1), dev_par)
    far_up = remote(9, rows(far, 1, 1), rows(far, 4, 1), dev_x[2])
    far_down = remote(10, rows(far, 3, 1), rows(far, 0, 1), dev_x[0])
    w_x = [
        remote(11 + j, wall.at[quarter_rows(nw, x)], wall.at[quarter_rows(nw, x)], dev_x[j])
        for j in range(3)
    ]
    w_yn = [
        remote(14 + j, wall.at[shard_rows(wa)], wall.at[shard_rows(wa)], dev_y[j]) for j in range(3)
    ]
    w_yf = [
        remote(17 + j, wall.at[shard_rows(nw)], wall.at[shard_rows(nw)], dev_y[j]) for j in range(3)
    ]
    w_c = [
        remote(20, wall.at[shard_rows(wa)], wall.at[shard_rows(wa)], dev_par),
        remote(21, wall.at[shard_rows(nw)], wall.at[shard_rows(nw)], dev_par),
    ]
    for j in range(3):
        near = lax.rem(wa + 4 * (3 - j), 16)
        w_c.append(remote(22 + j, wall.at[shard_rows(near)], wall.at[shard_rows(near)], dev_par))
    for j in range(3):
        other = lax.rem(nw + 4 * (3 - j), 16)
        w_c.append(remote(25 + j, wall.at[shard_rows(other)], wall.at[shard_rows(other)], dev_par))

    def ext_quarter(half, part):
        return wext.at[pl.ds(pl.multiple_of((2 * half + c) * SHARD + part * QUARTER, QUARTER), QUARTER)]

    def ext_shard(half):
        return wext.at[pl.ds(pl.multiple_of((2 * half + c) * SHARD, SHARD), SHARD)]

    def ext(send, recv, src, dst, device):
        return pltpu.make_async_remote_copy(
            src_ref=src,
            dst_ref=dst,
            send_sem=ssem_e.at[send],
            recv_sem=rsem_e.at[recv],
            device_id=device,
            device_id_type=MESH,
        )

    ext_t = ext(0, 0, wall.at[quarter_rows(wa, x)], ext_quarter(zh, x), dev_next)
    ext_z = ext(1, 1, wall.at[quarter_rows(wa, x)], ext_quarter(zh, x), dev_cross)
    ext_y_copies = [
        ext(2 + 2 * j + n, n, ext_quarter(half, x), ext_quarter(half, x), dev_y[j])
        for j in range(3)
        for n, half in ((0, zh), (1, 1 - zh))
    ]
    ext_x_copies = [
        ext(8 + 2 * j + n, 2 + 2 * j + n, ext_quarter(half, x), ext_quarter(half, x), dev_x[j])
        for j in range(3)
        for n, half in ((0, zh), (1, 1 - zh))
    ]
    ext_c_copies = [
        ext(14 + n, 8 + n, ext_shard(half), ext_shard(half), dev_par)
        for n, half in ((0, zh), (1, 1 - zh))
    ]

    w_z.start()

    @pl.when(is_end & (y == ext_y))
    def _():
        ext_t.start()
        ext_z.start()

    @pl.when(has_far)
    def _():
        far_a.start()

    @pl.when(is_direct)
    def _():
        far_b.start()

    @pl.when(is_via)
    def _():
        far_rows_b(own, dev_via).start()
        for head in passed:
            far_head(head, own, dev_via).start()

    up.start()
    down.start()
    par_mid.start()
    w_c[0].start()
    for copy in w_yn:
        copy.start()

    w_z.wait_recv()
    for copy in w_x:
        copy.start()
    up.wait_recv()
    par_bot.start()
    down.wait_recv()
    par_top.start()
    for copy in w_x:
        copy.wait_recv()
    w_c[1].start()
    for copy in w_yf:
        copy.start()

    @pl.when(is_next & (y == ext_y))
    def _():
        ext_t.wait_recv()
        ext_z.wait_recv()
        for copy in ext_y_copies:
            copy.start()

    par_mid.wait_recv()
    par_top.wait_recv()
    par_bot.wait_recv()
    load_q.wait()

    @pl.when(is_relay)
    def _():
        far_b.wait_recv()
        far_rows_b(far, dev_diag).start()

    scale = 1.0 / math.sqrt(HD)
    far_there = jnp.where(c == 0, wa > 0, wa < N_WA - 1)

    def biases(r, head, beside, there):
        radius_row = win_ref[0, head]
        radius_col = win_ref[1, head]
        out = []
        for gap in (-1, 0, 1):
            row = T_ROWS * x + r + gap
            ok = (row >= 0) & (row < N_HA * T_ROWS) & (abs(gap) <= radius_row)
            if beside:
                ok = ok & (radius_col >= 1) & there
            out.append(jnp.where(ok, 0.0, MASKED).astype(jnp.float32))
        return out

    def lanes(head):
        return pl.ds(pl.multiple_of(head * HD, HD), HD)

    def token_rows(r, count):
        return pl.ds(r * TOK if isinstance(r, int) else pl.multiple_of(r * TOK, TOK), count * TOK)

    def query_tile(r, head):
        part = pl.ds(r * HALF if isinstance(r, int) else pl.multiple_of(r * HALF, HALF), HALF)
        return jnp.concatenate([qry[0, part, lanes(head)], qry[1, part, lanes(head)]], axis=0)

    def scores(query, buf, r, head, bias):
        keys = buf[0, token_rows(r, 3), lanes(head)]
        raw = lax.dot_general(query, keys, NT, preferred_element_type=jnp.float32) * scale
        return [raw[:, j * TOK : (j + 1) * TOK] + bias[j] for j in range(3)]

    def values(weights, buf, r, head):
        return jnp.dot(
            jnp.concatenate(weights, axis=1).astype(jnp.bfloat16),
            buf[1, token_rows(r, 3), lanes(head)],
            preferred_element_type=jnp.float32,
        )

    def total(parts, op):
        out = parts[0]
        for part in parts[1:]:
            out = op(out, part)
        return out

    def near_tile(index, carry):
        r = index // HEADS_HERE
        head = lax.rem(index, HEADS_HERE)
        query = query_tile(r, head)
        s_own = scores(query, own, r, head, biases(r, head, False, True))
        s_par = scores(query, par, r, head, biases(r, head, True, True))
        highest = jnp.max(total(s_own + s_par, jnp.maximum), axis=1, keepdims=True)
        p_own = [jnp.exp(s - highest) for s in s_own]
        p_par = [jnp.exp(s - highest) for s in s_par]
        norm = jnp.sum(total(p_own + p_par, jnp.add), axis=1, keepdims=True)
        o_part[index] = values(p_own, own, r, head) + values(p_par, par, r, head)
        m_part[index] = jnp.broadcast_to(highest, (TOK, HD))
        l_part[index] = jnp.broadcast_to(norm, (TOK, HD))
        return carry

    lax.fori_loop(0, T_ROWS * HEADS_HERE, near_tile, 0)

    @pl.when(is_next)
    def _():
        @pl.when(y != ext_y)
        def _():
            for copy in ext_y_copies[:2]:
                copy.wait_recv()

        for copy in ext_x_copies:
            copy.start()

    @pl.when(has_far)
    def _():
        far_a.wait_send()
        for head in range(3):
            far_c[head].start()

    @pl.when(is_direct)
    def _():
        for head in passed:
            far_c[head].start()

    @pl.when(is_relay)
    def _():
        for head in passed:
            far_c[head].wait_recv()
            far_head(head, far, dev_diag).start()

    @pl.when(is_next)
    def _():
        for copy in ext_x_copies:
            copy.wait_recv()
        for copy in ext_c_copies:
            copy.start()

    @pl.when(has_far)
    def _():
        far_a.wait_recv()
        far_up.start()

    for j in range(3):
        w_yn[j].wait_recv()
        w_c[2 + j].start()

    @pl.when(has_far)
    def _():
        far_b.wait_recv()
        far_down.start()

    for j in range(3):
        w_yf[j].wait_recv()
        w_c[5 + j].start()

    @pl.when(has_far)
    def _():
        far_up.wait_recv()
        far_down.wait_recv()

    def far_tile(r, head):
        index = r * HEADS_HERE + head
        query = query_tile(r, head)
        s_far = scores(query, far, r, head, biases(r, head, True, far_there))
        before = m_part[index]
        highest = jnp.maximum(
            before, jnp.max(total(s_far, jnp.maximum), axis=1, keepdims=True)
        )
        shrink = jnp.exp(before - highest)
        p_far = [jnp.exp(s - highest) for s in s_far]
        norm = shrink * l_part[index] + jnp.sum(total(p_far, jnp.add), axis=1, keepdims=True)
        out = (shrink * o_part[index] + values(p_far, far, r, head)) / norm
        att[token_rows(r, 1), lanes(head)] = out.astype(jnp.bfloat16)

    def far_step(head, carry):
        @pl.when(has_far)
        def _():
            pltpu.make_async_remote_copy(
                src_ref=middle(own, 0),
                dst_ref=middle(far, 0),
                send_sem=ssem.at[28 + head],
                recv_sem=rsem.at[28 + head],
                device_id=dev_far,
                device_id_type=MESH,
            ).wait_recv()

        for r in range(T_ROWS):
            far_tile(r, head)
        return carry

    lax.fori_loop(0, HEADS_HERE, far_step, 0)
    for copy in w_c:
        copy.wait_recv()

    @pl.when(is_next)
    def _():
        for copy in ext_c_copies:
            copy.wait_recv()

    right = (x, wa, lax.rem(g + 1, N_TA))
    left = (x, wa, lax.rem(g + N_TA - 1, N_TA))

    def partial_sum(dest, r):
        weight = wall[pl.ds(pl.multiple_of(dest * FEAT, FEAT), FEAT), :]
        return lax.dot_general(
            att[token_rows(r, 1), :], weight, NT, preferred_element_type=jnp.float32
        )

    def extra_sum(taken, far_dest):
        weight = wext[pl.ds(pl.multiple_of(far_dest * FEAT, FEAT), FEAT), :]
        return lax.dot_general(taken, weight, NT, preferred_element_type=jnp.float32)

    def flow(slots, send, recv, device):
        def hop(src, k):
            return pltpu.make_async_remote_copy(
                src_ref=src,
                dst_ref=slots.at[k],
                send_sem=send.at[k],
                recv_sem=recv.at[k],
                device_id=device,
                device_id_type=MESH,
            )

        return hop

    hop_r = flow(slot_r, ssem_r, rsem_r, right)
    hop_l = flow(slot_l, ssem_l, rsem_l, left)

    def step(hop, slots, k, place, dest_of, ext_of):
        r = lax.rem(k, T_ROWS)
        taken = 2 * T_ROWS

        @pl.when((place == 0) & (k < T_ROWS))
        def _():
            hop(att.at[token_rows(r, 1)], k).start()

        @pl.when((place == 0) & (k >= taken))
        def _():
            slots[k] = partial_sum(dest_of(k), r).astype(jnp.bfloat16)
            hop(slots.at[k], k).start()

        @pl.when((place == 1) & (k < T_ROWS))
        def _():
            hop(slots.at[k], k).wait_recv()
            add = partial_sum(dest_of(k), r) + extra_sum(slots[k], ext_of(k))
            slots[N_PIECE - T_ROWS + r] = add.astype(jnp.bfloat16)
            hop(slots.at[N_PIECE - T_ROWS + r], k).start()

        @pl.when((place == 1) & (k >= T_ROWS) & (k < taken))
        def _():
            add = partial_sum(dest_of(k), r) + extra_sum(slots[r], ext_of(k))
            slots[k] = add.astype(jnp.bfloat16)
            hop(slots.at[k], k).start()

        @pl.when((place > 1) | ((place == 1) & (k >= taken)))
        def _():
            hop(slots.at[k], k).wait_recv()
            add = partial_sum(dest_of(k), r)
            slots[k] = (slots[k].astype(jnp.float32) + add).astype(jnp.bfloat16)
            hop(slots.at[k], k).start()

    def hops(tau, carry):
        k = tau - 2 * g

        @pl.when((k >= 0) & (k < T_ROWS * (N_TA - 1 - g)))
        def _():
            step(
                hop_r, slot_r, k, g, lambda m: N_TA - 1 - m // T_ROWS, lambda m: 1 - m // T_ROWS
            )

        n = tau - 2 * (N_TA - 1 - g)

        @pl.when((n >= 0) & (n < T_ROWS * g))
        def _():
            step(hop_l, slot_l, n, N_TA - 1 - g, lambda m: m // T_ROWS, lambda m: m // T_ROWS)

        return carry

    lax.fori_loop(0, T_ROWS * (N_TA - 1), hops, 0)

    load_h.wait()
    load_m.wait()
    gate, shift, gain = [mod[j, pl.ds(step_ref[0], 1), :] for j in range(3)]
    lane = lax.broadcasted_iota(jnp.int32, (TOK, HD), 1)

    def share(j, r):
        return pltpu.make_async_remote_copy(
            src_ref=stat.at[0, r],
            dst_ref=stat.at[j + 1, r],
            send_sem=ssem_s.at[j * T_ROWS + r],
            recv_sem=rsem_s.at[j * T_ROWS + r],
            device_id=dev_t[j],
            device_id_type=MESH,
        )

    for r in range(T_ROWS):
        own_part = partial_sum(g, r)
        k = T_ROWS * (N_TA - 1 - g) + r
        n = T_ROWS * g + r

        @pl.when(g > 0)
        def _():
            hop_r(slot_r.at[k], k).wait_recv()

        @pl.when(g < N_TA - 1)
        def _():
            hop_l(slot_l.at[n], n).wait_recv()

        projected = own_part + slot_r[k].astype(jnp.float32) + slot_l[n].astype(jnp.float32)
        part = pl.ds(r * HALF, HALF)
        before = jnp.concatenate([hid[0, part, :], hid[1, part, :]], axis=0).astype(jnp.float32)
        now = before + gate * projected
        mixed[pl.ds(r * TOK, TOK), :] = now
        rounded = now.astype(jnp.bfloat16)
        res_ref[0, part, :] = rounded[:HALF]
        res_ref[1, part, :] = rounded[HALF:]
        first = jnp.sum(now, axis=1, keepdims=True)
        second = jnp.sum(now * now, axis=1, keepdims=True)
        both = jnp.where(lane == 0, first, jnp.where(lane == 1, second, 0.0))
        stat[0, r] = jnp.transpose(both)[:8]
        for j in range(7):
            share(j, r).start()

    for r in range(T_ROWS):
        for j in range(7):
            share(j, r).wait_recv()
        line = total([stat[j, r] for j in range(N_TA)], jnp.add)
        column = jnp.transpose(jnp.concatenate([line] * (HD // 8), axis=0))
        average = column[:, 0:1] / D
        variance = column[:, 1:2] / D - average * average
        now = mixed[pl.ds(r * TOK, TOK), :]
        normed = (now - average) * lax.rsqrt(variance + EPSILON)
        out = (normed * (1.0 + gain) + shift).astype(jnp.bfloat16)
        part = pl.ds(r * HALF, HALF)
        ffn_ref[0, part, :] = out[:HALF]
        ffn_ref[1, part, :] = out[HALF:]

    for copy in [w_z, far_b, up, down, par_mid, par_top, par_bot]:
        copy.wait_send()
    for head in passed:
        far_c[head].wait_send()

    @pl.when(has_far)
    def _():
        for copy in [far_up, far_down] + far_c[:3]:
            copy.wait_send()

    for copy in w_x + w_yn + w_yf + w_c:
        copy.wait_send()
    for j in range(7):
        for r in range(T_ROWS):
            share(j, r).wait_send()

    @pl.when(is_end & (y == ext_y))
    def _():
        ext_t.wait_send()
        ext_z.wait_send()

    @pl.when(is_next)
    def _():
        @pl.when(y == ext_y)
        def _():
            for copy in ext_y_copies:
                copy.wait_send()

        for copy in ext_x_copies + ext_c_copies:
            copy.wait_send()

    def sent(k, carry):
        left_out = (k >= T_ROWS) & (k < 2 * T_ROWS)

        @pl.when((k < T_ROWS * (N_TA - 1 - g)) & ~((g == 0) & left_out))
        def _():
            hop_r(slot_r.at[k], k).wait_send()

        @pl.when((k < T_ROWS * g) & ~((g == N_TA - 1) & left_out))
        def _():
            hop_l(slot_l.at[k], k).wait_send()

        return carry

    lax.fori_loop(0, T_ROWS * (N_TA - 1), sent, 0)


def shards(hidden_states, queries, keys_values, out_weight, mod_table, windows, step_index):
    flat = (FRAMES, ROWS * COLS, FEAT)
    any_spec = pl.BlockSpec(memory_space=pl.ANY)
    smem_spec = pl.BlockSpec(memory_space=pltpu.SMEM)
    vmem_spec = pl.BlockSpec(memory_space=pltpu.VMEM)
    column = pltpu.VMEM((2, (T_ROWS + 2) * TOK, FEAT), jnp.bfloat16)
    tiles = T_ROWS * HEADS_HERE
    residual_out, ffn_input = pl.pallas_call(
        kernel,
        out_shape=[jax.ShapeDtypeStruct(flat, jnp.bfloat16)] * 2,
        in_specs=[smem_spec] * 2 + [any_spec] * 5,
        out_specs=[vmem_spec] * 2,
        scratch_shapes=[
            column,
            column,
            column,
            pltpu.VMEM((D, FEAT), jnp.bfloat16),
            pltpu.VMEM(flat, jnp.bfloat16),
            pltpu.VMEM(flat, jnp.bfloat16),
            pltpu.VMEM((3, mod_table.shape[0], FEAT), jnp.float32),
            pltpu.VMEM((TOKENS, FEAT), jnp.bfloat16),
            pltpu.VMEM((tiles, TOK, HD), jnp.float32),
            pltpu.VMEM((tiles, TOK, HD), jnp.float32),
            pltpu.VMEM((tiles, TOK, HD), jnp.float32),
            pltpu.VMEM((4 * SHARD, FEAT), jnp.bfloat16),
            pltpu.VMEM((N_PIECE, TOK, FEAT), jnp.bfloat16),
            pltpu.VMEM((N_PIECE, TOK, FEAT), jnp.bfloat16),
            pltpu.VMEM((TOKENS, FEAT), jnp.float32),
            pltpu.VMEM((N_TA, T_ROWS, 8, HD), jnp.float32),
            pltpu.SemaphoreType.DMA((10,)),
            pltpu.SemaphoreType.DMA((33,)),
            pltpu.SemaphoreType.DMA((33,)),
            pltpu.SemaphoreType.DMA((16,)),
            pltpu.SemaphoreType.DMA((10,)),
            pltpu.SemaphoreType.DMA((N_PIECE,)),
            pltpu.SemaphoreType.DMA((N_PIECE,)),
            pltpu.SemaphoreType.DMA((N_PIECE,)),
            pltpu.SemaphoreType.DMA((N_PIECE,)),
            pltpu.SemaphoreType.DMA((7 * T_ROWS,)),
            pltpu.SemaphoreType.DMA((7 * T_ROWS,)),
        ],
        compiler_params=pltpu.CompilerParams(
            collective_id=0, has_side_effects=True, vmem_limit_bytes=60 * 2**20
        ),
    )(
        windows.T,
        step_index,
        hidden_states.reshape(flat),
        queries.reshape(flat),
        keys_values.reshape((2,) + flat),
        out_weight.T,
        mod_table.transpose(1, 0, 2),
    )
    shape = (FRAMES, ROWS, COLS, FEAT)
    return residual_out.reshape(shape), ffn_input.reshape(shape)


def solution(mesh):
    return jax.shard_map(
        shards,
        mesh=mesh,
        in_specs=(
            P(None, "ha", "wa", "ta"),
            P(None, "ha", "wa", "ta"),
            P(None, None, "ha", "wa", "ta"),
            P("ta", "wa"),
            P(None, None, "ta"),
            P("ta", None),
            P(),
        ),
        out_specs=(P(None, "ha", "wa", "ta"), P(None, "ha", "wa", "ta")),
        check_vma=False,
    )
```

```python
import math

import jax
import jax.numpy as jnp
from jax import lax
from jax.experimental import pallas as pl
from jax.experimental.pallas import tpu as pltpu
from jax.sharding import PartitionSpec as P

D = 5120
HD = 128
TILE = 8
EPSILON = 1e-06

N_HA, N_WA, N_TA = 4, 16, 8
N_Y = 4
FRAMES, ROWS, COLS = 2, 24, 8
FEAT = 640
HEADS_HERE = 5
T_ROWS = ROWS // TILE
TOK = FRAMES * TILE * TILE
HALF = TILE * TILE
TOKENS = T_ROWS * TOK
SHARD = D // N_WA
QUARTER = SHARD // N_HA
N_PIECE = N_TA * T_ROWS
MASKED = -1e30
MESH = pl.DeviceIdType.MESH
NT = (((1,), (1,)), ((), ()))


def kernel(
    win_ref,
    step_ref,
    hid_ref,
    q_ref,
    kv_ref,
    wt_ref,
    mod_ref,
    res_ref,
    ffn_ref,
    own,
    par,
    far,
    wall,
    hid,
    qry,
    mod,
    att,
    o_part,
    m_part,
    l_part,
    w_far,
    slot_r,
    slot_l,
    mixed,
    stat,
    lsem,
    ssem,
    rsem,
    ssem_r,
    rsem_r,
    ssem_l,
    rsem_l,
    ssem_s,
    rsem_s,
):
    x = lax.axis_index("ha")
    wa = lax.axis_index("wa")
    g = lax.axis_index("ta")
    y = wa // 4
    zh = lax.rem(wa // 2, 2)
    c = lax.rem(wa, 2)
    nw = 4 * y + 2 * (1 - zh) + c

    dev_par = (x, 4 * y + 2 * zh + 1 - c, g)
    dev_far = (x, lax.rem(wa + 15 + 2 * c, 16), g)
    dev_z = (x, nw, g)
    dev_diag = (x, 4 * y + 2 * (1 - zh) + 1 - c, g)
    dev_via = (x, 15 * (wa // 8), g)
    dev_x = [(lax.rem(x + j + 1, N_HA), wa, g) for j in range(3)]
    dev_y = [(x, lax.rem(wa + 4 * (j + 1), 16), g) for j in range(3)]
    dev_t = [(x, wa, lax.rem(g + j + 1, N_TA)) for j in range(7)]

    def shard_rows(index):
        return pl.ds(pl.multiple_of(index * SHARD, SHARD), SHARD)

    def quarter_rows(index, part):
        return pl.ds(pl.multiple_of(index * SHARD + part * QUARTER, QUARTER), QUARTER)

    is_relay = (wa == 0) | (wa == N_WA - 1)
    has_far = (wa > 0) & (wa < N_WA - 1)
    is_via = (wa == 4) | (wa == 11)
    is_direct = has_far & (wa != 4) & (wa != 11)

    @pl.when(is_relay)
    def _():
        far[...] = jnp.zeros_like(far)

    barrier = pltpu.get_barrier_semaphore()
    peers = [dev_par, dev_far, dev_z, dev_diag] + dev_x + dev_y + dev_t
    for peer in peers:
        pl.semaphore_signal(barrier, inc=1, device_id=peer, device_id_type=MESH)

    loads = []
    for f in range(FRAMES):
        for r in range(T_ROWS):
            loads.append(
                pltpu.make_async_copy(
                    kv_ref.at[:, f, pl.ds(r * HALF, HALF), :],
                    own.at[:, pl.ds((r + 1) * TOK + f * HALF, HALF), :],
                    lsem.at[f * T_ROWS + r],
                )
            )
    load_w = pltpu.make_async_copy(wt_ref, wall.at[shard_rows(wa)], lsem.at[6])
    load_q = pltpu.make_async_copy(q_ref, qry, lsem.at[7])
    load_h = pltpu.make_async_copy(hid_ref, hid, lsem.at[8])
    load_m = pltpu.make_async_copy(mod_ref, mod, lsem.at[9])
    for load in loads:
        load.start()
    load_w.start()
    load_q.start()
    load_h.start()
    load_m.start()

    for load in loads:
        load.wait()
    load_w.wait()
    pl.semaphore_wait(barrier, len(peers))

    def remote(index, src, dst, device):
        return pltpu.make_async_remote_copy(
            src_ref=src,
            dst_ref=dst,
            send_sem=ssem.at[index],
            recv_sem=rsem.at[index],
            device_id=device,
            device_id_type=MESH,
        )

    def rows(buf, first, count):
        return buf.at[:, pl.ds(first * TOK, count * TOK), :]

    w_z = remote(0, wall.at[quarter_rows(wa, x)], wall.at[quarter_rows(wa, x)], dev_z)
    far_a = remote(1, rows(own, 1, 1), rows(far, 1, 1), dev_far)
    def far_rows_b(src, device):
        return remote(2, rows(src, 3, 1), rows(far, 3, 1), device)

    def middle(buf, which):
        return buf.at[which, pl.ds(2 * TOK, TOK), :]

    def far_rows_v(src, device):
        return remote(28, middle(src, 1), middle(far, 1), device)

    far_b = far_rows_b(own, dev_far)
    far_k = remote(3, middle(own, 0), middle(far, 0), dev_far)
    far_v = far_rows_v(own, dev_far)
    up = remote(4, rows(own, 1, 1), rows(own, 4, 1), dev_x[2])
    down = remote(5, rows(own, 3, 1), rows(own, 0, 1), dev_x[0])
    par_mid = remote(6, rows(own, 1, 3), rows(par, 1, 3), dev_par)
    par_top = remote(7, rows(own, 0, 1), rows(par, 0, 1), dev_par)
    par_bot = remote(8, rows(own, 4, 1), rows(par, 4, 1), dev_par)
    far_up = remote(9, rows(far, 1, 1), rows(far, 4, 1), dev_x[2])
    far_down = remote(10, rows(far, 3, 1), rows(far, 0, 1), dev_x[0])
    w_x = [
        remote(11 + j, wall.at[quarter_rows(nw, x)], wall.at[quarter_rows(nw, x)], dev_x[j])
        for j in range(3)
    ]
    w_yn = [
        remote(14 + j, wall.at[shard_rows(wa)], wall.at[shard_rows(wa)], dev_y[j]) for j in range(3)
    ]
    w_yf = [
        remote(17 + j, wall.at[shard_rows(nw)], wall.at[shard_rows(nw)], dev_y[j]) for j in range(3)
    ]
    w_c = [
        remote(20, wall.at[shard_rows(wa)], wall.at[shard_rows(wa)], dev_par),
        remote(21, wall.at[shard_rows(nw)], wall.at[shard_rows(nw)], dev_par),
    ]
    for j in range(3):
        near = lax.rem(wa + 4 * (3 - j), 16)
        w_c.append(remote(22 + j, wall.at[shard_rows(near)], wall.at[shard_rows(near)], dev_par))
    for j in range(3):
        other = lax.rem(nw + 4 * (3 - j), 16)
        w_c.append(remote(25 + j, wall.at[shard_rows(other)], wall.at[shard_rows(other)], dev_par))

    w_z.start()

    @pl.when(has_far)
    def _():
        far_a.start()

    @pl.when(is_direct)
    def _():
        far_b.start()

    @pl.when(is_via)
    def _():
        far_rows_b(own, dev_via).start()
        far_rows_v(own, dev_via).start()

    up.start()
    down.start()
    par_mid.start()
    w_c[0].start()
    for copy in w_yn:
        copy.start()

    w_z.wait_recv()
    for copy in w_x:
        copy.start()
    up.wait_recv()
    par_bot.start()
    down.wait_recv()
    par_top.start()
    for copy in w_x:
        copy.wait_recv()
    w_c[1].start()
    for copy in w_yf:
        copy.start()

    @pl.when(g == 0)
    def _():
        slot_r[...] = jnp.zeros_like(slot_r)

    @pl.when(g == N_TA - 1)
    def _():
        slot_l[...] = jnp.zeros_like(slot_l)

    par_mid.wait_recv()
    par_top.wait_recv()
    par_bot.wait_recv()
    load_q.wait()

    @pl.when(is_relay)
    def _():
        far_b.wait_recv()
        far_rows_b(far, dev_diag).start()

    scale = 1.0 / math.sqrt(HD)
    far_there = jnp.where(c == 0, wa > 0, wa < N_WA - 1)

    def biases(r, head, beside, there):
        radius_row = win_ref[0, head]
        radius_col = win_ref[1, head]
        out = []
        for gap in (-1, 0, 1):
            row = T_ROWS * x + r + gap
            ok = (row >= 0) & (row < N_HA * T_ROWS) & (abs(gap) <= radius_row)
            if beside:
                ok = ok & (radius_col >= 1) & there
            out.append(jnp.where(ok, 0.0, MASKED).astype(jnp.float32))
        return out

    def lanes(head):
        return pl.ds(pl.multiple_of(head * HD, HD), HD)

    def token_rows(r, count):
        return pl.ds(r * TOK if isinstance(r, int) else pl.multiple_of(r * TOK, TOK), count * TOK)

    def query_tile(r, head):
        part = pl.ds(r * HALF if isinstance(r, int) else pl.multiple_of(r * HALF, HALF), HALF)
        return jnp.concatenate([qry[0, part, lanes(head)], qry[1, part, lanes(head)]], axis=0)

    def scores(query, buf, r, head, bias):
        keys = buf[0, token_rows(r, 3), lanes(head)]
        raw = lax.dot_general(query, keys, NT, preferred_element_type=jnp.float32) * scale
        return [raw[:, j * TOK : (j + 1) * TOK] + bias[j] for j in range(3)]

    def values(weights, buf, r, head):
        return jnp.dot(
            jnp.concatenate(weights, axis=1).astype(jnp.bfloat16),
            buf[1, token_rows(r, 3), lanes(head)],
            preferred_element_type=jnp.float32,
        )

    def total(parts, op):
        out = parts[0]
        for part in parts[1:]:
            out = op(out, part)
        return out

    def near_tile(index, carry):
        r = index // HEADS_HERE
        head = lax.rem(index, HEADS_HERE)
        query = query_tile(r, head)
        s_own = scores(query, own, r, head, biases(r, head, False, True))
        s_par = scores(query, par, r, head, biases(r, head, True, True))
        highest = jnp.max(total(s_own + s_par, jnp.maximum), axis=1, keepdims=True)
        p_own = [jnp.exp(s - highest) for s in s_own]
        p_par = [jnp.exp(s - highest) for s in s_par]
        norm = jnp.sum(total(p_own + p_par, jnp.add), axis=1, keepdims=True)
        o_part[index] = values(p_own, own, r, head) + values(p_par, par, r, head)
        m_part[index] = jnp.broadcast_to(highest, (TOK, HD))
        l_part[index] = jnp.broadcast_to(norm, (TOK, HD))
        return carry

    lax.fori_loop(0, T_ROWS * HEADS_HERE, near_tile, 0)

    @pl.when(has_far)
    def _():
        far_a.wait_send()
        far_k.start()

    @pl.when(is_relay)
    def _():
        far_v.wait_recv()
        far_rows_v(far, dev_diag).start()

    @pl.when(has_far)
    def _():
        far_a.wait_recv()
        far_up.start()

    for j in range(3):
        w_yn[j].wait_recv()
        w_c[2 + j].start()

    @pl.when(has_far)
    def _():
        far_b.wait_recv()
        far_down.start()

    for j in range(3):
        w_yf[j].wait_recv()
        w_c[5 + j].start()

    @pl.when(is_direct)
    def _():
        far_k.wait_send()
        far_v.start()

    @pl.when(has_far)
    def _():
        far_up.wait_recv()
        far_down.wait_recv()
        far_k.wait_recv()

    def far_weights(index, carry):
        r = index // HEADS_HERE
        head = lax.rem(index, HEADS_HERE)
        query = query_tile(r, head)
        s_far = scores(query, far, r, head, biases(r, head, True, far_there))
        before = m_part[index]
        highest = jnp.maximum(before, jnp.max(total(s_far, jnp.maximum), axis=1, keepdims=True))
        shrink = jnp.exp(before - highest)
        p_far = [jnp.exp(s - highest) for s in s_far]
        norm = shrink * l_part[index] + jnp.sum(total(p_far, jnp.add), axis=1, keepdims=True)
        share_of = 1.0 / norm
        o_part[index] = o_part[index] * (shrink * share_of)
        for j in range(3):
            w_far[index, :, j * TOK : (j + 1) * TOK] = (p_far[j] * share_of).astype(jnp.bfloat16)
        return carry

    lax.fori_loop(0, T_ROWS * HEADS_HERE, far_weights, 0)

    @pl.when(has_far)
    def _():
        far_v.wait_recv()

    def far_values(head, carry):
        for r in range(T_ROWS):
            index = r * HEADS_HERE + head
            out = o_part[index] + jnp.dot(
                w_far[index],
                far[1, token_rows(r, 3), lanes(head)],
                preferred_element_type=jnp.float32,
            )
            att[token_rows(r, 1), lanes(head)] = out.astype(jnp.bfloat16)
        return carry

    lax.fori_loop(0, HEADS_HERE, far_values, 0)
    for copy in w_c:
        copy.wait_recv()

    right = (x, wa, lax.rem(g + 1, N_TA))
    left = (x, wa, lax.rem(g + N_TA - 1, N_TA))

    def partial_sum(dest, r):
        weight = wall[pl.ds(pl.multiple_of(dest * FEAT, FEAT), FEAT), :]
        return lax.dot_general(
            att[token_rows(r, 1), :], weight, NT, preferred_element_type=jnp.float32
        )

    def hop_r(k):
        return pltpu.make_async_remote_copy(
            src_ref=slot_r.at[k],
            dst_ref=slot_r.at[k],
            send_sem=ssem_r.at[k],
            recv_sem=rsem_r.at[k],
            device_id=right,
            device_id_type=MESH,
        )

    def hop_l(k):
        return pltpu.make_async_remote_copy(
            src_ref=slot_l.at[k],
            dst_ref=slot_l.at[k],
            send_sem=ssem_l.at[k],
            recv_sem=rsem_l.at[k],
            device_id=left,
            device_id_type=MESH,
        )

    def hop(tau, carry):
        k = tau - 2 * g

        @pl.when((k >= 0) & (k < T_ROWS * (N_TA - 1 - g)))
        def _():
            @pl.when(g > 0)
            def _():
                hop_r(k).wait_recv()

            add = partial_sum(N_TA - 1 - k // T_ROWS, lax.rem(k, T_ROWS))
            slot_r[k] = (slot_r[k].astype(jnp.float32) + add).astype(jnp.bfloat16)
            hop_r(k).start()

        n = tau - 2 * (N_TA - 1 - g)

        @pl.when((n >= 0) & (n < T_ROWS * g))
        def _():
            @pl.when(g < N_TA - 1)
            def _():
                hop_l(n).wait_recv()

            add = partial_sum(n // T_ROWS, lax.rem(n, T_ROWS))
            slot_l[n] = (slot_l[n].astype(jnp.float32) + add).astype(jnp.bfloat16)
            hop_l(n).start()

        return carry

    lax.fori_loop(0, T_ROWS * (N_TA - 1), hop, 0)

    load_h.wait()
    load_m.wait()
    gate, shift, gain = [mod[j, pl.ds(step_ref[0], 1), :] for j in range(3)]
    lane = lax.broadcasted_iota(jnp.int32, (TOK, HD), 1)

    def share(j, r):
        return pltpu.make_async_remote_copy(
            src_ref=stat.at[0, r],
            dst_ref=stat.at[j + 1, r],
            send_sem=ssem_s.at[j * T_ROWS + r],
            recv_sem=rsem_s.at[j * T_ROWS + r],
            device_id=dev_t[j],
            device_id_type=MESH,
        )

    for r in range(T_ROWS):
        own_part = partial_sum(g, r)
        k = T_ROWS * (N_TA - 1 - g) + r
        n = T_ROWS * g + r

        @pl.when(g > 0)
        def _():
            hop_r(k).wait_recv()

        @pl.when(g < N_TA - 1)
        def _():
            hop_l(n).wait_recv()

        projected = own_part + slot_r[k].astype(jnp.float32) + slot_l[n].astype(jnp.float32)
        part = pl.ds(r * HALF, HALF)
        before = jnp.concatenate([hid[0, part, :], hid[1, part, :]], axis=0).astype(jnp.float32)
        now = before + gate * projected
        mixed[pl.ds(r * TOK, TOK), :] = now
        rounded = now.astype(jnp.bfloat16)
        res_ref[0, part, :] = rounded[:HALF]
        res_ref[1, part, :] = rounded[HALF:]
        first = jnp.sum(now, axis=1, keepdims=True)
        second = jnp.sum(now * now, axis=1, keepdims=True)
        both = jnp.where(lane == 0, first, jnp.where(lane == 1, second, 0.0))
        stat[0, r] = jnp.transpose(both)[:8]
        for j in range(7):
            share(j, r).start()

    for r in range(T_ROWS):
        for j in range(7):
            share(j, r).wait_recv()
        line = total([stat[j, r] for j in range(N_TA)], jnp.add)
        column = jnp.transpose(jnp.concatenate([line] * (HD // 8), axis=0))
        average = column[:, 0:1] / D
        variance = column[:, 1:2] / D - average * average
        now = mixed[pl.ds(r * TOK, TOK), :]
        normed = (now - average) * lax.rsqrt(variance + EPSILON)
        out = (normed * (1.0 + gain) + shift).astype(jnp.bfloat16)
        part = pl.ds(r * HALF, HALF)
        ffn_ref[0, part, :] = out[:HALF]
        ffn_ref[1, part, :] = out[HALF:]

    for copy in [w_z, far_b, far_v, up, down, par_mid, par_top, par_bot]:
        copy.wait_send()

    @pl.when(has_far)
    def _():
        far_up.wait_send()
        far_down.wait_send()

    @pl.when(is_via)
    def _():
        far_k.wait_send()

    for copy in w_x + w_yn + w_yf + w_c:
        copy.wait_send()
    for j in range(7):
        for r in range(T_ROWS):
            share(j, r).wait_send()

    def sent(k, carry):
        @pl.when(k < T_ROWS * (N_TA - 1 - g))
        def _():
            hop_r(k).wait_send()

        @pl.when(k < T_ROWS * g)
        def _():
            hop_l(k).wait_send()

        return carry

    lax.fori_loop(0, T_ROWS * (N_TA - 1), sent, 0)


def shards(hidden_states, queries, keys_values, out_weight, mod_table, windows, step_index):
    flat = (FRAMES, ROWS * COLS, FEAT)
    any_spec = pl.BlockSpec(memory_space=pl.ANY)
    smem_spec = pl.BlockSpec(memory_space=pltpu.SMEM)
    vmem_spec = pl.BlockSpec(memory_space=pltpu.VMEM)
    column = pltpu.VMEM((2, (T_ROWS + 2) * TOK, FEAT), jnp.bfloat16)
    tiles = T_ROWS * HEADS_HERE
    residual_out, ffn_input = pl.pallas_call(
        kernel,
        out_shape=[jax.ShapeDtypeStruct(flat, jnp.bfloat16)] * 2,
        in_specs=[smem_spec] * 2 + [any_spec] * 5,
        out_specs=[vmem_spec] * 2,
        scratch_shapes=[
            column,
            column,
            column,
            pltpu.VMEM((D, FEAT), jnp.bfloat16),
            pltpu.VMEM(flat, jnp.bfloat16),
            pltpu.VMEM(flat, jnp.bfloat16),
            pltpu.VMEM((3, mod_table.shape[0], FEAT), jnp.float32),
            pltpu.VMEM((TOKENS, FEAT), jnp.bfloat16),
            pltpu.VMEM((tiles, TOK, HD), jnp.float32),
            pltpu.VMEM((tiles, TOK, HD), jnp.float32),
            pltpu.VMEM((tiles, TOK, HD), jnp.float32),
            pltpu.VMEM((tiles, TOK, 3 * TOK), jnp.bfloat16),
            pltpu.VMEM((N_PIECE, TOK, FEAT), jnp.bfloat16),
            pltpu.VMEM((N_PIECE, TOK, FEAT), jnp.bfloat16),
            pltpu.VMEM((TOKENS, FEAT), jnp.float32),
            pltpu.VMEM((N_TA, T_ROWS, 8, HD), jnp.float32),
            pltpu.SemaphoreType.DMA((10,)),
            pltpu.SemaphoreType.DMA((29,)),
            pltpu.SemaphoreType.DMA((29,)),
            pltpu.SemaphoreType.DMA((N_PIECE,)),
            pltpu.SemaphoreType.DMA((N_PIECE,)),
            pltpu.SemaphoreType.DMA((N_PIECE,)),
            pltpu.SemaphoreType.DMA((N_PIECE,)),
            pltpu.SemaphoreType.DMA((7 * T_ROWS,)),
            pltpu.SemaphoreType.DMA((7 * T_ROWS,)),
        ],
        compiler_params=pltpu.CompilerParams(
            collective_id=0, has_side_effects=True, vmem_limit_bytes=60 * 2**20
        ),
    )(
        windows.T,
        step_index,
        hidden_states.reshape(flat),
        queries.reshape(flat),
        keys_values.reshape((2,) + flat),
        out_weight.T,
        mod_table.transpose(1, 0, 2),
    )
    shape = (FRAMES, ROWS, COLS, FEAT)
    return residual_out.reshape(shape), ffn_input.reshape(shape)


def solution(mesh):
    return jax.shard_map(
        shards,
        mesh=mesh,
        in_specs=(
            P(None, "ha", "wa", "ta"),
            P(None, "ha", "wa", "ta"),
            P(None, None, "ha", "wa", "ta"),
            P("ta", "wa"),
            P(None, None, "ta"),
            P("ta", None),
            P(),
        ),
        out_specs=(P(None, "ha", "wa", "ta"), P(None, "ha", "wa", "ta")),
        check_vma=False,
    )
```

```python
import math

import jax
import jax.numpy as jnp
from jax import lax
from jax.experimental import pallas as pl
from jax.experimental.pallas import tpu as pltpu
from jax.sharding import PartitionSpec as P

D = 5120
HD = 128
TILE = 8
EPSILON = 1e-06

N_HA, N_WA, N_TA = 4, 16, 8
N_Y = 4
FRAMES, ROWS, COLS = 2, 24, 8
FEAT = 640
HEADS_HERE = 5
T_ROWS = ROWS // TILE
TOK = FRAMES * TILE * TILE
HALF = TILE * TILE
TOKENS = T_ROWS * TOK
SHARD = D // N_WA
QUARTER = SHARD // N_HA
N_PIECE = N_TA * T_ROWS
MASKED = -1e30
MESH = pl.DeviceIdType.MESH
NT = (((1,), (1,)), ((), ()))


def kernel(
    win_ref,
    step_ref,
    hid_ref,
    q_ref,
    kv_ref,
    wt_ref,
    mod_ref,
    res_ref,
    ffn_ref,
    own,
    par,
    far,
    wall,
    hid,
    qry,
    mod,
    att,
    o_part,
    m_part,
    l_part,
    w_far,
    slot_r,
    slot_l,
    mixed,
    stat,
    lsem,
    ssem,
    rsem,
    ssem_r,
    rsem_r,
    ssem_l,
    rsem_l,
    ssem_s,
    rsem_s,
):
    x = lax.axis_index("ha")
    wa = lax.axis_index("wa")
    g = lax.axis_index("ta")
    y = wa // 4
    zh = lax.rem(wa // 2, 2)
    c = lax.rem(wa, 2)
    nw = 4 * y + 2 * (1 - zh) + c

    dev_par = (x, 4 * y + 2 * zh + 1 - c, g)
    dev_far = (x, lax.rem(wa + 15 + 2 * c, 16), g)
    dev_z = (x, nw, g)
    dev_diag = (x, 4 * y + 2 * (1 - zh) + 1 - c, g)
    dev_via = (x, 15 * (wa // 8), g)
    dev_x = [(lax.rem(x + j + 1, N_HA), wa, g) for j in range(3)]
    dev_y = [(x, lax.rem(wa + 4 * (j + 1), 16), g) for j in range(3)]
    dev_t = [(x, wa, lax.rem(g + j + 1, N_TA)) for j in range(7)]

    def shard_rows(index):
        return pl.ds(pl.multiple_of(index * SHARD, SHARD), SHARD)

    def quarter_rows(index, part):
        return pl.ds(pl.multiple_of(index * SHARD + part * QUARTER, QUARTER), QUARTER)

    is_relay = (wa == 0) | (wa == N_WA - 1)
    has_far = (wa > 0) & (wa < N_WA - 1)
    is_via = (wa == 4) | (wa == 11)
    is_direct = has_far & (wa != 4) & (wa != 11)

    @pl.when(is_relay)
    def _():
        far[...] = jnp.zeros_like(far)

    barrier = pltpu.get_barrier_semaphore()
    peers = [dev_par, dev_far, dev_z, dev_diag] + dev_x + dev_y + dev_t
    for peer in peers:
        pl.semaphore_signal(barrier, inc=1, device_id=peer, device_id_type=MESH)

    loads = []
    for f in range(FRAMES):
        for r in range(T_ROWS):
            loads.append(
                pltpu.make_async_copy(
                    kv_ref.at[:, f, pl.ds(r * HALF, HALF), :],
                    own.at[:, pl.ds((r + 1) * TOK + f * HALF, HALF), :],
                    lsem.at[f * T_ROWS + r],
                )
            )
    load_w = pltpu.make_async_copy(wt_ref, wall.at[shard_rows(wa)], lsem.at[6])
    load_q = pltpu.make_async_copy(q_ref, qry, lsem.at[7])
    load_h = pltpu.make_async_copy(hid_ref, hid, lsem.at[8])
    load_m = pltpu.make_async_copy(mod_ref, mod, lsem.at[9])
    for load in loads:
        load.start()
    load_w.start()
    load_q.start()
    load_h.start()
    load_m.start()

    for load in loads:
        load.wait()
    load_w.wait()
    pl.semaphore_wait(barrier, len(peers))

    def remote(index, src, dst, device):
        return pltpu.make_async_remote_copy(
            src_ref=src,
            dst_ref=dst,
            send_sem=ssem.at[index],
            recv_sem=rsem.at[index],
            device_id=device,
            device_id_type=MESH,
        )

    def rows(buf, first, count):
        return buf.at[:, pl.ds(first * TOK, count * TOK), :]

    w_z = remote(0, wall.at[quarter_rows(wa, x)], wall.at[quarter_rows(wa, x)], dev_z)
    far_a = remote(1, rows(own, 1, 1), rows(far, 1, 1), dev_far)
    def far_rows_b(src, device):
        return remote(2, rows(src, 3, 1), rows(far, 3, 1), device)

    def middle(buf, which):
        return buf.at[which, pl.ds(2 * TOK, TOK), :]

    def far_rows_v(src, device):
        return remote(28, middle(src, 1), middle(far, 1), device)

    far_b = far_rows_b(own, dev_far)
    far_k = remote(3, middle(own, 0), middle(far, 0), dev_far)
    far_v = far_rows_v(own, dev_far)
    up = remote(4, rows(own, 1, 1), rows(own, 4, 1), dev_x[2])
    down = remote(5, rows(own, 3, 1), rows(own, 0, 1), dev_x[0])
    par_mid = remote(6, rows(own, 1, 3), rows(par, 1, 3), dev_par)
    par_top = remote(7, rows(own, 0, 1), rows(par, 0, 1), dev_par)
    par_bot = remote(8, rows(own, 4, 1), rows(par, 4, 1), dev_par)
    far_up = remote(9, rows(far, 1, 1), rows(far, 4, 1), dev_x[2])
    far_down = remote(10, rows(far, 3, 1), rows(far, 0, 1), dev_x[0])
    w_x = [
        remote(11 + j, wall.at[quarter_rows(nw, x)], wall.at[quarter_rows(nw, x)], dev_x[j])
        for j in range(3)
    ]
    w_yn = [
        remote(14 + j, wall.at[shard_rows(wa)], wall.at[shard_rows(wa)], dev_y[j]) for j in range(3)
    ]
    w_yf = [
        remote(17 + j, wall.at[shard_rows(nw)], wall.at[shard_rows(nw)], dev_y[j]) for j in range(3)
    ]
    w_c = [
        remote(20, wall.at[shard_rows(wa)], wall.at[shard_rows(wa)], dev_par),
        remote(21, wall.at[shard_rows(nw)], wall.at[shard_rows(nw)], dev_par),
    ]
    for j in range(3):
        near = lax.rem(wa + 4 * (3 - j), 16)
        w_c.append(remote(22 + j, wall.at[shard_rows(near)], wall.at[shard_rows(near)], dev_par))
    for j in range(3):
        other = lax.rem(nw + 4 * (3 - j), 16)
        w_c.append(remote(25 + j, wall.at[shard_rows(other)], wall.at[shard_rows(other)], dev_par))

    w_z.start()

    @pl.when(has_far)
    def _():
        far_a.start()

    @pl.when(is_direct)
    def _():
        far_b.start()

    @pl.when(is_via)
    def _():
        far_rows_b(own, dev_via).start()
        far_rows_v(own, dev_via).start()

    up.start()
    down.start()
    par_mid.start()
    w_c[0].start()
    for copy in w_yn:
        copy.start()

    w_z.wait_recv()
    for copy in w_x:
        copy.start()
    up.wait_recv()
    par_bot.start()
    down.wait_recv()
    par_top.start()
    for copy in w_x:
        copy.wait_recv()
    w_c[1].start()
    for copy in w_yf:
        copy.start()

    @pl.when(g == 0)
    def _():
        slot_r[...] = jnp.zeros_like(slot_r)

    @pl.when(g == N_TA - 1)
    def _():
        slot_l[...] = jnp.zeros_like(slot_l)

    par_mid.wait_recv()
    par_top.wait_recv()
    par_bot.wait_recv()
    load_q.wait()

    @pl.when(is_relay)
    def _():
        far_b.wait_recv()
        far_rows_b(far, dev_diag).start()

    scale = 1.0 / math.sqrt(HD)
    far_there = jnp.where(c == 0, wa > 0, wa < N_WA - 1)

    def biases(r, head, beside, there):
        radius_row = win_ref[0, head]
        radius_col = win_ref[1, head]
        out = []
        for gap in (-1, 0, 1):
            row = T_ROWS * x + r + gap
            ok = (row >= 0) & (row < N_HA * T_ROWS) & (abs(gap) <= radius_row)
            if beside:
                ok = ok & (radius_col >= 1) & there
            out.append(jnp.where(ok, 0.0, MASKED).astype(jnp.float32))
        return out

    def lanes(head):
        return pl.ds(head * HD if isinstance(head, int) else pl.multiple_of(head * HD, HD), HD)

    def token_rows(r, count):
        return pl.ds(r * TOK if isinstance(r, int) else pl.multiple_of(r * TOK, TOK), count * TOK)

    def query_tile(r, head):
        part = pl.ds(r * HALF if isinstance(r, int) else pl.multiple_of(r * HALF, HALF), HALF)
        return jnp.concatenate([qry[0, part, lanes(head)], qry[1, part, lanes(head)]], axis=0)

    def scores(query, buf, r, head, bias):
        keys = buf[0, token_rows(r, 3), lanes(head)]
        raw = lax.dot_general(query, keys, NT, preferred_element_type=jnp.float32) * scale
        return [raw[:, j * TOK : (j + 1) * TOK] + bias[j] for j in range(3)]

    def values(weights, buf, r, head):
        return jnp.dot(
            jnp.concatenate(weights, axis=1).astype(jnp.bfloat16),
            buf[1, token_rows(r, 3), lanes(head)],
            preferred_element_type=jnp.float32,
        )

    def total(parts, op):
        out = parts[0]
        for part in parts[1:]:
            out = op(out, part)
        return out

    def near_tile(index, carry):
        r = index // HEADS_HERE
        head = lax.rem(index, HEADS_HERE)
        query = query_tile(r, head)
        s_own = scores(query, own, r, head, biases(r, head, False, True))
        s_par = scores(query, par, r, head, biases(r, head, True, True))
        highest = jnp.max(total(s_own + s_par, jnp.maximum), axis=1, keepdims=True)
        p_own = [jnp.exp(s - highest) for s in s_own]
        p_par = [jnp.exp(s - highest) for s in s_par]
        norm = jnp.sum(total(p_own + p_par, jnp.add), axis=1, keepdims=True)
        o_part[index] = values(p_own, own, r, head) + values(p_par, par, r, head)
        m_part[index] = jnp.broadcast_to(highest, (TOK, HD))
        l_part[index] = jnp.broadcast_to(norm, (TOK, HD))
        return carry

    lax.fori_loop(0, T_ROWS * HEADS_HERE, near_tile, 0)

    @pl.when(has_far)
    def _():
        far_a.wait_send()
        far_k.start()

    @pl.when(is_relay)
    def _():
        far_v.wait_recv()
        far_rows_v(far, dev_diag).start()

    @pl.when(has_far)
    def _():
        far_a.wait_recv()
        far_up.start()

    for j in range(3):
        w_yn[j].wait_recv()
        w_c[2 + j].start()

    @pl.when(has_far)
    def _():
        far_b.wait_recv()
        far_down.start()

    for j in range(3):
        w_yf[j].wait_recv()
        w_c[5 + j].start()

    @pl.when(is_direct)
    def _():
        far_k.wait_send()
        far_v.start()

    @pl.when(has_far)
    def _():
        far_up.wait_recv()
        far_down.wait_recv()
        far_k.wait_recv()

    def far_weights(index, carry):
        r = index // HEADS_HERE
        head = lax.rem(index, HEADS_HERE)
        query = query_tile(r, head)
        s_far = scores(query, far, r, head, biases(r, head, True, far_there))
        before = m_part[index]
        highest = jnp.maximum(before, jnp.max(total(s_far, jnp.maximum), axis=1, keepdims=True))
        shrink = jnp.exp(before - highest)
        p_far = [jnp.exp(s - highest) for s in s_far]
        norm = shrink * l_part[index] + jnp.sum(total(p_far, jnp.add), axis=1, keepdims=True)
        share_of = 1.0 / norm
        o_part[index] = o_part[index] * (shrink * share_of)
        for j in range(3):
            w_far[index, :, j * TOK : (j + 1) * TOK] = (p_far[j] * share_of).astype(jnp.bfloat16)
        return carry

    lax.fori_loop(0, T_ROWS * HEADS_HERE, far_weights, 0)

    @pl.when(has_far)
    def _():
        far_v.wait_recv()

    for copy in w_c:
        copy.wait_recv()

    right = (x, wa, lax.rem(g + 1, N_TA))
    left = (x, wa, lax.rem(g + N_TA - 1, N_TA))

    def partial_sum(dest, r):
        weight = wall[pl.ds(pl.multiple_of(dest * FEAT, FEAT), FEAT), :]
        return lax.dot_general(
            att[token_rows(r, 1), :], weight, NT, preferred_element_type=jnp.float32
        )

    def hop_r(k):
        return pltpu.make_async_remote_copy(
            src_ref=slot_r.at[k],
            dst_ref=slot_r.at[k],
            send_sem=ssem_r.at[k],
            recv_sem=rsem_r.at[k],
            device_id=right,
            device_id_type=MESH,
        )

    def hop_l(k):
        return pltpu.make_async_remote_copy(
            src_ref=slot_l.at[k],
            dst_ref=slot_l.at[k],
            send_sem=ssem_l.at[k],
            recv_sem=rsem_l.at[k],
            device_id=left,
            device_id_type=MESH,
        )

    def hop(tau, carry):
        k = tau - T_ROWS * g

        @pl.when((k >= 0) & (k < T_ROWS * (N_TA - 1 - g)))
        def _():
            @pl.when(g > 0)
            def _():
                hop_r(k).wait_recv()

            add = partial_sum(N_TA - 1 - k // T_ROWS, lax.rem(k, T_ROWS))
            slot_r[k] = (slot_r[k].astype(jnp.float32) + add).astype(jnp.bfloat16)
            hop_r(k).start()

        n = tau - T_ROWS * (N_TA - 1 - g)

        @pl.when((n >= 0) & (n < T_ROWS * g))
        def _():
            @pl.when(g < N_TA - 1)
            def _():
                hop_l(n).wait_recv()

            add = partial_sum(n // T_ROWS, lax.rem(n, T_ROWS))
            slot_l[n] = (slot_l[n].astype(jnp.float32) + add).astype(jnp.bfloat16)
            hop_l(n).start()

        return carry

    def finish_row(r, carry):
        for head in range(HEADS_HERE):
            index = r * HEADS_HERE + head
            out = o_part[index] + jnp.dot(
                w_far[index],
                far[1, token_rows(r, 3), lanes(head)],
                preferred_element_type=jnp.float32,
            )
            att[token_rows(r, 1), lanes(head)] = out.astype(jnp.bfloat16)
        return hop(r, carry)

    lax.fori_loop(0, T_ROWS, finish_row, 0)
    lax.fori_loop(T_ROWS, T_ROWS * (N_TA - 1), hop, 0)

    load_h.wait()
    load_m.wait()
    gate, shift, gain = [mod[j, pl.ds(step_ref[0], 1), :] for j in range(3)]
    lane = lax.broadcasted_iota(jnp.int32, (TOK, HD), 1)

    def share(j, r):
        return pltpu.make_async_remote_copy(
            src_ref=stat.at[0, r],
            dst_ref=stat.at[j + 1, r],
            send_sem=ssem_s.at[j * T_ROWS + r],
            recv_sem=rsem_s.at[j * T_ROWS + r],
            device_id=dev_t[j],
            device_id_type=MESH,
        )

    for r in range(T_ROWS):
        own_part = partial_sum(g, r)
        k = T_ROWS * (N_TA - 1 - g) + r
        n = T_ROWS * g + r

        @pl.when(g > 0)
        def _():
            hop_r(k).wait_recv()

        @pl.when(g < N_TA - 1)
        def _():
            hop_l(n).wait_recv()

        projected = own_part + slot_r[k].astype(jnp.float32) + slot_l[n].astype(jnp.float32)
        part = pl.ds(r * HALF, HALF)
        before = jnp.concatenate([hid[0, part, :], hid[1, part, :]], axis=0).astype(jnp.float32)
        now = before + gate * projected
        mixed[pl.ds(r * TOK, TOK), :] = now
        rounded = now.astype(jnp.bfloat16)
        res_ref[0, part, :] = rounded[:HALF]
        res_ref[1, part, :] = rounded[HALF:]
        first = jnp.sum(now, axis=1, keepdims=True)
        second = jnp.sum(now * now, axis=1, keepdims=True)
        both = jnp.where(lane == 0, first, jnp.where(lane == 1, second, 0.0))
        stat[0, r] = jnp.transpose(both)[:8]
        for j in range(7):
            share(j, r).start()

    for r in range(T_ROWS):
        for j in range(7):
            share(j, r).wait_recv()
        line = total([stat[j, r] for j in range(N_TA)], jnp.add)
        column = jnp.transpose(jnp.concatenate([line] * (HD // 8), axis=0))
        average = column[:, 0:1] / D
        variance = column[:, 1:2] / D - average * average
        now = mixed[pl.ds(r * TOK, TOK), :]
        normed = (now - average) * lax.rsqrt(variance + EPSILON)
        out = (normed * (1.0 + gain) + shift).astype(jnp.bfloat16)
        part = pl.ds(r * HALF, HALF)
        ffn_ref[0, part, :] = out[:HALF]
        ffn_ref[1, part, :] = out[HALF:]

    for copy in [w_z, far_b, far_v, up, down, par_mid, par_top, par_bot]:
        copy.wait_send()

    @pl.when(has_far)
    def _():
        far_up.wait_send()
        far_down.wait_send()

    @pl.when(is_via)
    def _():
        far_k.wait_send()

    for copy in w_x + w_yn + w_yf + w_c:
        copy.wait_send()
    for j in range(7):
        for r in range(T_ROWS):
            share(j, r).wait_send()

    def sent(k, carry):
        @pl.when(k < T_ROWS * (N_TA - 1 - g))
        def _():
            hop_r(k).wait_send()

        @pl.when(k < T_ROWS * g)
        def _():
            hop_l(k).wait_send()

        return carry

    lax.fori_loop(0, T_ROWS * (N_TA - 1), sent, 0)


def shards(hidden_states, queries, keys_values, out_weight, mod_table, windows, step_index):
    flat = (FRAMES, ROWS * COLS, FEAT)
    any_spec = pl.BlockSpec(memory_space=pl.ANY)
    smem_spec = pl.BlockSpec(memory_space=pltpu.SMEM)
    vmem_spec = pl.BlockSpec(memory_space=pltpu.VMEM)
    column = pltpu.VMEM((2, (T_ROWS + 2) * TOK, FEAT), jnp.bfloat16)
    tiles = T_ROWS * HEADS_HERE
    residual_out, ffn_input = pl.pallas_call(
        kernel,
        out_shape=[jax.ShapeDtypeStruct(flat, jnp.bfloat16)] * 2,
        in_specs=[smem_spec] * 2 + [any_spec] * 5,
        out_specs=[vmem_spec] * 2,
        scratch_shapes=[
            column,
            column,
            column,
            pltpu.VMEM((D, FEAT), jnp.bfloat16),
            pltpu.VMEM(flat, jnp.bfloat16),
            pltpu.VMEM(flat, jnp.bfloat16),
            pltpu.VMEM((3, mod_table.shape[0], FEAT), jnp.float32),
            pltpu.VMEM((TOKENS, FEAT), jnp.bfloat16),
            pltpu.VMEM((tiles, TOK, HD), jnp.float32),
            pltpu.VMEM((tiles, TOK, HD), jnp.float32),
            pltpu.VMEM((tiles, TOK, HD), jnp.float32),
            pltpu.VMEM((tiles, TOK, 3 * TOK), jnp.bfloat16),
            pltpu.VMEM((N_PIECE, TOK, FEAT), jnp.bfloat16),
            pltpu.VMEM((N_PIECE, TOK, FEAT), jnp.bfloat16),
            pltpu.VMEM((TOKENS, FEAT), jnp.float32),
            pltpu.VMEM((N_TA, T_ROWS, 8, HD), jnp.float32),
            pltpu.SemaphoreType.DMA((10,)),
            pltpu.SemaphoreType.DMA((29,)),
            pltpu.SemaphoreType.DMA((29,)),
            pltpu.SemaphoreType.DMA((N_PIECE,)),
            pltpu.SemaphoreType.DMA((N_PIECE,)),
            pltpu.SemaphoreType.DMA((N_PIECE,)),
            pltpu.SemaphoreType.DMA((N_PIECE,)),
            pltpu.SemaphoreType.DMA((7 * T_ROWS,)),
            pltpu.SemaphoreType.DMA((7 * T_ROWS,)),
        ],
        compiler_params=pltpu.CompilerParams(
            collective_id=0, has_side_effects=True, vmem_limit_bytes=60 * 2**20
        ),
    )(
        windows.T,
        step_index,
        hidden_states.reshape(flat),
        queries.reshape(flat),
        keys_values.reshape((2,) + flat),
        out_weight.T,
        mod_table.transpose(1, 0, 2),
    )
    shape = (FRAMES, ROWS, COLS, FEAT)
    return residual_out.reshape(shape), ffn_input.reshape(shape)


def solution(mesh):
    return jax.shard_map(
        shards,
        mesh=mesh,
        in_specs=(
            P(None, "ha", "wa", "ta"),
            P(None, "ha", "wa", "ta"),
            P(None, None, "ha", "wa", "ta"),
            P("ta", "wa"),
            P(None, None, "ta"),
            P("ta", None),
            P(),
        ),
        out_specs=(P(None, "ha", "wa", "ta"), P(None, "ha", "wa", "ta")),
        check_vma=False,
    )
```

```python
import math

import jax
import jax.numpy as jnp
from jax import lax
from jax.experimental import pallas as pl
from jax.experimental.pallas import tpu as pltpu
from jax.sharding import PartitionSpec as P

D = 5120
HD = 128
TILE = 8
EPSILON = 1e-06

N_HA, N_WA, N_TA = 4, 16, 8
N_Y = 4
FRAMES, ROWS, COLS = 2, 24, 8
FEAT = 640
HEADS_HERE = 5
T_ROWS = ROWS // TILE
TOK = FRAMES * TILE * TILE
HALF = TILE * TILE
TOKENS = T_ROWS * TOK
SHARD = D // N_WA
QUARTER = SHARD // N_HA
N_PIECE = N_TA * T_ROWS
MASKED = -1e30
MESH = pl.DeviceIdType.MESH
NT = (((1,), (1,)), ((), ()))


def kernel(
    win_ref,
    step_ref,
    hid_ref,
    q_ref,
    kv_ref,
    wt_ref,
    mod_ref,
    res_ref,
    ffn_ref,
    own,
    par,
    far,
    wall,
    hid,
    qry,
    mod,
    att,
    o_part,
    m_part,
    l_part,
    w_far,
    slot_r,
    slot_l,
    mixed,
    stat,
    lsem,
    ssem,
    rsem,
    ssem_r,
    rsem_r,
    ssem_l,
    rsem_l,
    ssem_s,
    rsem_s,
):
    x = lax.axis_index("ha")
    wa = lax.axis_index("wa")
    g = lax.axis_index("ta")
    y = wa // 4
    zh = lax.rem(wa // 2, 2)
    c = lax.rem(wa, 2)
    nw = 4 * y + 2 * (1 - zh) + c

    dev_par = (x, 4 * y + 2 * zh + 1 - c, g)
    dev_far = (x, lax.rem(wa + 15 + 2 * c, 16), g)
    dev_z = (x, nw, g)
    dev_diag = (x, 4 * y + 2 * (1 - zh) + 1 - c, g)
    dev_via = (x, 15 * (wa // 8), g)
    dev_x = [(lax.rem(x + j + 1, N_HA), wa, g) for j in range(3)]
    dev_y = [(x, lax.rem(wa + 4 * (j + 1), 16), g) for j in range(3)]
    dev_t = [(x, wa, lax.rem(g + j + 1, N_TA)) for j in range(7)]

    def shard_rows(index):
        return pl.ds(pl.multiple_of(index * SHARD, SHARD), SHARD)

    def quarter_rows(index, part):
        return pl.ds(pl.multiple_of(index * SHARD + part * QUARTER, QUARTER), QUARTER)

    is_relay = (wa == 0) | (wa == N_WA - 1)
    has_far = (wa > 0) & (wa < N_WA - 1)
    is_via = (wa == 4) | (wa == 11)
    is_direct = has_far & (wa != 4) & (wa != 11)

    @pl.when(is_relay)
    def _():
        far[...] = jnp.zeros_like(far)

    barrier = pltpu.get_barrier_semaphore()
    peers = [dev_par, dev_far, dev_z, dev_diag] + dev_x + dev_y + dev_t
    for peer in peers:
        pl.semaphore_signal(barrier, inc=1, device_id=peer, device_id_type=MESH)

    loads = []
    for f in range(FRAMES):
        for r in range(T_ROWS):
            loads.append(
                pltpu.make_async_copy(
                    kv_ref.at[:, f, pl.ds(r * HALF, HALF), :],
                    own.at[:, pl.ds((r + 1) * TOK + f * HALF, HALF), :],
                    lsem.at[f * T_ROWS + r],
                )
            )
    load_w = pltpu.make_async_copy(wt_ref, wall.at[shard_rows(wa)], lsem.at[6])
    load_q = pltpu.make_async_copy(q_ref, qry, lsem.at[7])
    load_h = pltpu.make_async_copy(hid_ref, hid, lsem.at[8])
    load_m = pltpu.make_async_copy(mod_ref, mod, lsem.at[9])
    for load in loads:
        load.start()
    load_w.start()
    load_q.start()
    load_h.start()
    load_m.start()

    for load in loads:
        load.wait()
    load_w.wait()
    pl.semaphore_wait(barrier, len(peers))

    def remote(index, src, dst, device):
        return pltpu.make_async_remote_copy(
            src_ref=src,
            dst_ref=dst,
            send_sem=ssem.at[index],
            recv_sem=rsem.at[index],
            device_id=device,
            device_id_type=MESH,
        )

    def rows(buf, first, count):
        return buf.at[:, pl.ds(first * TOK, count * TOK), :]

    w_z = remote(0, wall.at[quarter_rows(wa, x)], wall.at[quarter_rows(wa, x)], dev_z)
    far_a = remote(1, rows(own, 1, 1), rows(far, 1, 1), dev_far)
    def far_rows_b(src, device):
        return remote(2, rows(src, 3, 1), rows(far, 3, 1), device)

    def middle(buf, which):
        return buf.at[which, pl.ds(2 * TOK, TOK), :]

    def far_rows_v(src, device):
        return remote(28, middle(src, 1), middle(far, 1), device)

    far_b = far_rows_b(own, dev_far)
    far_k = remote(3, middle(own, 0), middle(far, 0), dev_far)
    far_v = far_rows_v(own, dev_far)
    up = remote(4, rows(own, 1, 1), rows(own, 4, 1), dev_x[2])
    down = remote(5, rows(own, 3, 1), rows(own, 0, 1), dev_x[0])
    par_mid = remote(6, rows(own, 1, 3), rows(par, 1, 3), dev_par)
    par_top = remote(7, rows(own, 0, 1), rows(par, 0, 1), dev_par)
    par_bot = remote(8, rows(own, 4, 1), rows(par, 4, 1), dev_par)
    far_up = remote(9, rows(far, 1, 1), rows(far, 4, 1), dev_x[2])
    far_down = remote(10, rows(far, 3, 1), rows(far, 0, 1), dev_x[0])
    w_x = [
        remote(11 + j, wall.at[quarter_rows(nw, x)], wall.at[quarter_rows(nw, x)], dev_x[j])
        for j in range(3)
    ]
    w_yn = [
        remote(14 + j, wall.at[shard_rows(wa)], wall.at[shard_rows(wa)], dev_y[j]) for j in range(3)
    ]
    w_yf = [
        remote(17 + j, wall.at[shard_rows(nw)], wall.at[shard_rows(nw)], dev_y[j]) for j in range(3)
    ]
    w_c = [
        remote(20, wall.at[shard_rows(wa)], wall.at[shard_rows(wa)], dev_par),
        remote(21, wall.at[shard_rows(nw)], wall.at[shard_rows(nw)], dev_par),
    ]
    for j in range(3):
        near = lax.rem(wa + 4 * (3 - j), 16)
        w_c.append(remote(22 + j, wall.at[shard_rows(near)], wall.at[shard_rows(near)], dev_par))
    for j in range(3):
        other = lax.rem(nw + 4 * (3 - j), 16)
        w_c.append(remote(25 + j, wall.at[shard_rows(other)], wall.at[shard_rows(other)], dev_par))

    w_z.start()

    @pl.when(has_far)
    def _():
        far_a.start()

    @pl.when(is_direct)
    def _():
        far_b.start()

    @pl.when(is_via)
    def _():
        far_rows_b(own, dev_via).start()
        far_rows_v(own, dev_via).start()

    up.start()
    down.start()
    par_mid.start()
    w_c[0].start()
    for copy in w_yn:
        copy.start()

    w_z.wait_recv()
    for copy in w_x:
        copy.start()
    up.wait_recv()
    par_bot.start()
    down.wait_recv()
    par_top.start()
    for copy in w_x:
        copy.wait_recv()
    w_c[1].start()
    for copy in w_yf:
        copy.start()

    @pl.when(g == 0)
    def _():
        slot_r[...] = jnp.zeros_like(slot_r)

    @pl.when(g == N_TA - 1)
    def _():
        slot_l[...] = jnp.zeros_like(slot_l)

    par_mid.wait_recv()
    par_top.wait_recv()
    par_bot.wait_recv()
    load_q.wait()

    @pl.when(is_relay)
    def _():
        far_b.wait_recv()
        far_rows_b(far, dev_diag).start()

    scale = 1.0 / math.sqrt(HD)
    far_there = jnp.where(c == 0, wa > 0, wa < N_WA - 1)

    def biases(r, head, beside, there):
        radius_row = win_ref[0, head]
        radius_col = win_ref[1, head]
        out = []
        for gap in (-1, 0, 1):
            row = T_ROWS * x + r + gap
            ok = (row >= 0) & (row < N_HA * T_ROWS) & (abs(gap) <= radius_row)
            if beside:
                ok = ok & (radius_col >= 1) & there
            out.append(jnp.where(ok, 0.0, MASKED).astype(jnp.float32))
        return out

    def lanes(head):
        return pl.ds(head * HD if isinstance(head, int) else pl.multiple_of(head * HD, HD), HD)

    def token_rows(r, count):
        return pl.ds(r * TOK if isinstance(r, int) else pl.multiple_of(r * TOK, TOK), count * TOK)

    def query_tile(r, head):
        part = pl.ds(r * HALF if isinstance(r, int) else pl.multiple_of(r * HALF, HALF), HALF)
        return jnp.concatenate([qry[0, part, lanes(head)], qry[1, part, lanes(head)]], axis=0)

    def scores(query, buf, r, head, bias):
        keys = buf[0, token_rows(r, 3), lanes(head)]
        raw = lax.dot_general(query, keys, NT, preferred_element_type=jnp.float32) * scale
        return [raw[:, j * TOK : (j + 1) * TOK] + bias[j] for j in range(3)]

    def values(weights, buf, r, head):
        return jnp.dot(
            jnp.concatenate(weights, axis=1).astype(jnp.bfloat16),
            buf[1, token_rows(r, 3), lanes(head)],
            preferred_element_type=jnp.float32,
        )

    def total(parts, op):
        out = parts[0]
        for part in parts[1:]:
            out = op(out, part)
        return out

    def near_tile(index, carry):
        r = index // HEADS_HERE
        head = lax.rem(index, HEADS_HERE)
        query = query_tile(r, head)
        s_own = scores(query, own, r, head, biases(r, head, False, True))
        s_par = scores(query, par, r, head, biases(r, head, True, True))
        highest = jnp.max(total(s_own + s_par, jnp.maximum), axis=1, keepdims=True)
        p_own = [jnp.exp(s - highest) for s in s_own]
        p_par = [jnp.exp(s - highest) for s in s_par]
        norm = jnp.sum(total(p_own + p_par, jnp.add), axis=1, keepdims=True)
        o_part[index] = values(p_own, own, r, head) + values(p_par, par, r, head)
        m_part[index] = jnp.broadcast_to(highest, (TOK, HD))
        l_part[index] = jnp.broadcast_to(norm, (TOK, HD))
        return carry

    lax.fori_loop(0, T_ROWS * HEADS_HERE, near_tile, 0)

    @pl.when(has_far)
    def _():
        far_a.wait_send()
        far_k.start()

    @pl.when(is_relay)
    def _():
        far_v.wait_recv()
        far_rows_v(far, dev_diag).start()

    @pl.when(has_far)
    def _():
        far_a.wait_recv()
        far_up.start()

    for j in range(3):
        w_yn[j].wait_recv()
        w_c[2 + j].start()

    @pl.when(has_far)
    def _():
        far_b.wait_recv()
        far_down.start()

    @pl.when(is_direct)
    def _():
        far_k.wait_send()
        far_v.start()

    for j in range(3):
        w_yf[j].wait_recv()
        w_c[5 + j].start()

    @pl.when(has_far)
    def _():
        far_up.wait_recv()
        far_down.wait_recv()
        far_k.wait_recv()

    def far_weights(index, carry):
        r = index // HEADS_HERE
        head = lax.rem(index, HEADS_HERE)
        query = query_tile(r, head)
        s_far = scores(query, far, r, head, biases(r, head, True, far_there))
        before = m_part[index]
        highest = jnp.maximum(before, jnp.max(total(s_far, jnp.maximum), axis=1, keepdims=True))
        shrink = jnp.exp(before - highest)
        p_far = [jnp.exp(s - highest) for s in s_far]
        norm = shrink * l_part[index] + jnp.sum(total(p_far, jnp.add), axis=1, keepdims=True)
        share_of = 1.0 / norm
        o_part[index] = o_part[index] * (shrink * share_of)
        for j in range(3):
            w_far[index, :, j * TOK : (j + 1) * TOK] = (p_far[j] * share_of).astype(jnp.bfloat16)
        return carry

    lax.fori_loop(0, T_ROWS * HEADS_HERE, far_weights, 0)

    @pl.when(has_far)
    def _():
        far_v.wait_recv()

    for copy in w_c:
        copy.wait_recv()

    right = (x, wa, lax.rem(g + 1, N_TA))
    left = (x, wa, lax.rem(g + N_TA - 1, N_TA))

    def partial_sum(dest, r):
        weight = wall[pl.ds(pl.multiple_of(dest * FEAT, FEAT), FEAT), :]
        return lax.dot_general(
            att[token_rows(r, 1), :], weight, NT, preferred_element_type=jnp.float32
        )

    def hop_r(k):
        return pltpu.make_async_remote_copy(
            src_ref=slot_r.at[k],
            dst_ref=slot_r.at[k],
            send_sem=ssem_r.at[k],
            recv_sem=rsem_r.at[k],
            device_id=right,
            device_id_type=MESH,
        )

    def hop_l(k):
        return pltpu.make_async_remote_copy(
            src_ref=slot_l.at[k],
            dst_ref=slot_l.at[k],
            send_sem=ssem_l.at[k],
            recv_sem=rsem_l.at[k],
            device_id=left,
            device_id_type=MESH,
        )

    def hop(tau, carry):
        k = tau - T_ROWS * g

        @pl.when((k >= 0) & (k < T_ROWS * (N_TA - 1 - g)))
        def _():
            @pl.when(g > 0)
            def _():
                hop_r(k).wait_recv()

            add = partial_sum(N_TA - 1 - k // T_ROWS, lax.rem(k, T_ROWS))
            slot_r[k] = (slot_r[k].astype(jnp.float32) + add).astype(jnp.bfloat16)
            hop_r(k).start()

        n = tau - T_ROWS * (N_TA - 1 - g)

        @pl.when((n >= 0) & (n < T_ROWS * g))
        def _():
            @pl.when(g < N_TA - 1)
            def _():
                hop_l(n).wait_recv()

            add = partial_sum(n // T_ROWS, lax.rem(n, T_ROWS))
            slot_l[n] = (slot_l[n].astype(jnp.float32) + add).astype(jnp.bfloat16)
            hop_l(n).start()

        return carry

    def finish_row(r, carry):
        for head in range(HEADS_HERE):
            index = r * HEADS_HERE + head
            out = o_part[index] + jnp.dot(
                w_far[index],
                far[1, token_rows(r, 3), lanes(head)],
                preferred_element_type=jnp.float32,
            )
            att[token_rows(r, 1), lanes(head)] = out.astype(jnp.bfloat16)
        return hop(r, carry)

    lax.fori_loop(0, T_ROWS, finish_row, 0)
    lax.fori_loop(T_ROWS, T_ROWS * (N_TA - 1), hop, 0)

    load_h.wait()
    load_m.wait()
    gate, shift, gain = [mod[j, pl.ds(step_ref[0], 1), :] for j in range(3)]
    lane = lax.broadcasted_iota(jnp.int32, (TOK, HD), 1)

    def share(j, r):
        return pltpu.make_async_remote_copy(
            src_ref=stat.at[0, r],
            dst_ref=stat.at[j + 1, r],
            send_sem=ssem_s.at[j * T_ROWS + r],
            recv_sem=rsem_s.at[j * T_ROWS + r],
            device_id=dev_t[j],
            device_id_type=MESH,
        )

    for r in range(T_ROWS):
        own_part = partial_sum(g, r)
        k = T_ROWS * (N_TA - 1 - g) + r
        n = T_ROWS * g + r

        @pl.when(g > 0)
        def _():
            hop_r(k).wait_recv()

        @pl.when(g < N_TA - 1)
        def _():
            hop_l(n).wait_recv()

        projected = own_part + slot_r[k].astype(jnp.float32) + slot_l[n].astype(jnp.float32)
        part = pl.ds(r * HALF, HALF)
        before = jnp.concatenate([hid[0, part, :], hid[1, part, :]], axis=0).astype(jnp.float32)
        now = before + gate * projected
        mixed[pl.ds(r * TOK, TOK), :] = now
        rounded = now.astype(jnp.bfloat16)
        res_ref[0, part, :] = rounded[:HALF]
        res_ref[1, part, :] = rounded[HALF:]
        first = jnp.sum(now, axis=1, keepdims=True)
        second = jnp.sum(now * now, axis=1, keepdims=True)
        both = jnp.where(lane == 0, first, jnp.where(lane == 1, second, 0.0))
        stat[0, r] = jnp.transpose(both)[:8]
        for j in range(7):
            share(j, r).start()

    for r in range(T_ROWS):
        for j in range(7):
            share(j, r).wait_recv()
        line = total([stat[j, r] for j in range(N_TA)], jnp.add)
        column = jnp.transpose(jnp.concatenate([line] * (HD // 8), axis=0))
        average = column[:, 0:1] / D
        variance = column[:, 1:2] / D - average * average
        now = mixed[pl.ds(r * TOK, TOK), :]
        normed = (now - average) * lax.rsqrt(variance + EPSILON)
        out = (normed * (1.0 + gain) + shift).astype(jnp.bfloat16)
        part = pl.ds(r * HALF, HALF)
        ffn_ref[0, part, :] = out[:HALF]
        ffn_ref[1, part, :] = out[HALF:]

    for copy in [w_z, far_b, far_v, up, down, par_mid, par_top, par_bot]:
        copy.wait_send()

    @pl.when(has_far)
    def _():
        far_up.wait_send()
        far_down.wait_send()

    @pl.when(is_via)
    def _():
        far_k.wait_send()

    for copy in w_x + w_yn + w_yf + w_c:
        copy.wait_send()
    for j in range(7):
        for r in range(T_ROWS):
            share(j, r).wait_send()

    def sent(k, carry):
        @pl.when(k < T_ROWS * (N_TA - 1 - g))
        def _():
            hop_r(k).wait_send()

        @pl.when(k < T_ROWS * g)
        def _():
            hop_l(k).wait_send()

        return carry

    lax.fori_loop(0, T_ROWS * (N_TA - 1), sent, 0)


def shards(hidden_states, queries, keys_values, out_weight, mod_table, windows, step_index):
    flat = (FRAMES, ROWS * COLS, FEAT)
    any_spec = pl.BlockSpec(memory_space=pl.ANY)
    smem_spec = pl.BlockSpec(memory_space=pltpu.SMEM)
    vmem_spec = pl.BlockSpec(memory_space=pltpu.VMEM)
    column = pltpu.VMEM((2, (T_ROWS + 2) * TOK, FEAT), jnp.bfloat16)
    tiles = T_ROWS * HEADS_HERE
    residual_out, ffn_input = pl.pallas_call(
        kernel,
        out_shape=[jax.ShapeDtypeStruct(flat, jnp.bfloat16)] * 2,
        in_specs=[smem_spec] * 2 + [any_spec] * 5,
        out_specs=[vmem_spec] * 2,
        scratch_shapes=[
            column,
            column,
            column,
            pltpu.VMEM((D, FEAT), jnp.bfloat16),
            pltpu.VMEM(flat, jnp.bfloat16),
            pltpu.VMEM(flat, jnp.bfloat16),
            pltpu.VMEM((3, mod_table.shape[0], FEAT), jnp.float32),
            pltpu.VMEM((TOKENS, FEAT), jnp.bfloat16),
            pltpu.VMEM((tiles, TOK, HD), jnp.float32),
            pltpu.VMEM((tiles, TOK, HD), jnp.float32),
            pltpu.VMEM((tiles, TOK, HD), jnp.float32),
            pltpu.VMEM((tiles, TOK, 3 * TOK), jnp.bfloat16),
            pltpu.VMEM((N_PIECE, TOK, FEAT), jnp.bfloat16),
            pltpu.VMEM((N_PIECE, TOK, FEAT), jnp.bfloat16),
            pltpu.VMEM((TOKENS, FEAT), jnp.float32),
            pltpu.VMEM((N_TA, T_ROWS, 8, HD), jnp.float32),
            pltpu.SemaphoreType.DMA((10,)),
            pltpu.SemaphoreType.DMA((29,)),
            pltpu.SemaphoreType.DMA((29,)),
            pltpu.SemaphoreType.DMA((N_PIECE,)),
            pltpu.SemaphoreType.DMA((N_PIECE,)),
            pltpu.SemaphoreType.DMA((N_PIECE,)),
            pltpu.SemaphoreType.DMA((N_PIECE,)),
            pltpu.SemaphoreType.DMA((7 * T_ROWS,)),
            pltpu.SemaphoreType.DMA((7 * T_ROWS,)),
        ],
        compiler_params=pltpu.CompilerParams(
            collective_id=0, has_side_effects=True, vmem_limit_bytes=60 * 2**20
        ),
    )(
        windows.T,
        step_index,
        hidden_states.reshape(flat),
        queries.reshape(flat),
        keys_values.reshape((2,) + flat),
        out_weight.T,
        mod_table.transpose(1, 0, 2),
    )
    shape = (FRAMES, ROWS, COLS, FEAT)
    return residual_out.reshape(shape), ffn_input.reshape(shape)


def solution(mesh):
    return jax.shard_map(
        shards,
        mesh=mesh,
        in_specs=(
            P(None, "ha", "wa", "ta"),
            P(None, "ha", "wa", "ta"),
            P(None, None, "ha", "wa", "ta"),
            P("ta", "wa"),
            P(None, None, "ta"),
            P("ta", None),
            P(),
        ),
        out_specs=(P(None, "ha", "wa", "ta"), P(None, "ha", "wa", "ta")),
        check_vma=False,
    )
```
